512 devices in a mesh: gy: 16 (over x, y), gx: 32 (over z, core).
Axes of the slice: x: 4, y: 4, z: 16, core: 2. Of those that a mesh axis runs over, the one named last changes fastest.
Arguments:
- cost_volume: int32 [256, 512, 256], P('gy', 'gx'), may hold values from 0 to 64
- left_image: float32 [256, 512], P('gy', 'gx'), may hold values from -6 to 6
- p_small: int32 [4], replicated, may hold values from 4 to 16
- p_large: int32 [4], replicated, may hold values from 32 to 128
Outputs:
- aggregated: float32 [256, 512, 256], P('gy', 'gx')
The draws below stay inside these ranges and needn't reach their ends.
Inputs may be any that keep to these rules, and one draw needn't show every extreme that they name: `p_small`: every small penalty is below every large penalty.
All inputs are finite; a program needn't handle non-finite values.
Results may differ from the reference program's by a relative error of at most 0.00002.
Values sent between devices are 32-bit elements; how exact they have to be, the bound alone decides.
No kernel may reach another device: no remote copies, remote signals or barrier semaphores. Data moves between devices by JAX's collectives and lax.ppermute only.
A program may use at most 64 MiB of HBM per device.

```python
from functools import partial
import jax
import jax.numpy as jnp
from jax import lax

DSP = 256
H = 256
W = 512


def draw_cost_volume(key, part):
    subkeys = jax.random.split(jax.random.fold_in(key, 11), 10)
    row_index = jnp.arange(H, dtype=jnp.int32)[:, None]
    column_index = jnp.arange(W, dtype=jnp.int32)[None, :]
    stripe_span = jax.random.randint(subkeys[0], (), W * 3 // 8, W // 2 + 1, dtype=jnp.int32)
    stripe_start = jax.random.randint(subkeys[1], (), W // 8, W - stripe_span - W // 8 + 1, dtype=jnp.int32)
    band_span = jax.random.randint(subkeys[2], (), H * 3 // 8, H // 2 + 1, dtype=jnp.int32)
    band_start = jax.random.randint(subkeys[3], (), H // 8, H - band_span - H // 8 + 1, dtype=jnp.int32)
    in_stripe = jnp.logical_and(column_index >= stripe_start, column_index < stripe_start + stripe_span)
    in_band = jnp.logical_and(row_index >= band_start, row_index < band_start + band_span)
    untextured = jnp.logical_or(in_stripe, in_band)
    slope_cols = jax.random.randint(subkeys[4], (), -(DSP // 2), DSP // 2 + 1, dtype=jnp.int32)
    slope_rows = jax.random.randint(subkeys[5], (), -(DSP // 2), DSP // 2 + 1, dtype=jnp.int32)
    shift_base = jax.random.randint(subkeys[6], (), 0, DSP, dtype=jnp.int32)
    jitter = jax.random.randint(subkeys[7], (H, W), -1, 2, dtype=jnp.int32)
    surface = jnp.mod(shift_base + slope_cols * column_index // W + slope_rows * row_index // H + jitter, DSP)
    labels = jnp.arange(DSP, dtype=jnp.int32)
    distance = jnp.minimum(jnp.abs(labels[None, None, :] - surface[:, :, None]), 10)
    textured = jnp.minimum(jax.random.randint(subkeys[8], (H, W, DSP), 0, 25, dtype=jnp.int32) + 4 * distance, 64)
    plateau = jax.random.randint(subkeys[9], (H, W), 8, 57, dtype=jnp.int32)
    return jnp.where(untextured[:, :, None], plateau[:, :, None], textured).astype(jnp.int32)


def with_ends(drawn, key, smallest, largest):
    shape = drawn.shape
    place = [jax.random.randint(jax.random.fold_in(key, axis), (), 0, shape[axis]) for axis in range(len(shape))]
    drawn = drawn.at[tuple(place)].set(smallest)
    longest = shape.index(max(shape))
    place[longest] = (place[longest] + 1) % shape[longest]
    return drawn.at[tuple(place)].set(largest)


def steps_of(own_key, extent, cuts, least, top_value):
    gain, own = 1.0, jax.random.fold_in(own_key, 6)
    for axis_at, parts in cuts:
        steps = jnp.exp(jax.random.uniform(jax.random.fold_in(own, axis_at), (parts,), jnp.float32, least / len(cuts), top_value / len(cuts)))
        gain = gain * jnp.repeat(steps, extent[axis_at] // parts).reshape([-1 if axis == axis_at else 1 for axis in range(len(extent))])
    return gain


def gaussian(own_key, dims, spread, limit, shards=(), kind=jnp.bfloat16):
    gain = steps_of(own_key, dims, shards, -0.22, 0.18) if shards else 1.0
    array = jax.random.normal(own_key, dims, jnp.float32) * spread * gain
    return jnp.minimum(jnp.maximum(array, -limit), limit).astype(kind)


def setup_inputs(seed: int = 0) -> dict:
    key_list = jax.random.split(jax.random.key(seed), 5)
    cost_volume = draw_cost_volume(jax.random.fold_in(key_list[4], 71), 0)
    left_image = gaussian(key_list[1], (H, W), 1.0, 6.0, ((0, 16), (1, 32)), jnp.float32)
    p_small = with_ends(jax.random.randint(key_list[2], (4,), 4, 17), jax.random.fold_in(key_list[2], 1), 4, 16).astype(jnp.int32)
    p_large = with_ends(jax.random.randint(key_list[3], (4,), 32, 129), jax.random.fold_in(key_list[3], 1), 32, 128).astype(jnp.int32)
    return {"cost_volume": cost_volume, "left_image": left_image, "p_small": p_small, "p_large": p_large}


FAR = 1.0e30
GRADIENT_GAIN = 4.0
OUT_SCALE = 1.0 / 256.0


def advance(previous, inputs, penalty_one):
    cost_line, large_line = inputs
    lowest = jnp.min(previous, axis=-1, keepdims=True)
    padded = jnp.pad(previous, ((0, 0), (1, 1)), constant_values=FAR)
    neighbour = jnp.minimum(padded[:, :-2], padded[:, 2:]) + penalty_one
    chosen = jnp.minimum(jnp.minimum(previous, neighbour), lowest + large_line[:, None])
    updated = cost_line.astype(jnp.float32) + chosen - lowest
    return updated, updated


def sweep(cost_lines, large_lines, penalty_one, start, backward):
    boundary, path_part = lax.scan(partial(advance, penalty_one=penalty_one), start, (cost_lines, large_lines), reverse=backward)
    return path_part, boundary


def adaptive(penalty_one, penalty_two, step_diff):
    return penalty_one + (penalty_two - penalty_one) / (1.0 + GRADIENT_GAIN * jnp.abs(step_diff))


def reference(cost_volume, left_image, p_small, p_large):
    padded = jnp.pad(left_image, 1)
    middle = padded[1:-1, 1:-1]
    small_pens = p_small.astype(jnp.float32)
    large_pens = p_large.astype(jnp.float32)
    penalty_right = adaptive(small_pens[0], large_pens[0], middle - padded[1:-1, :-2]).T
    penalty_left = adaptive(small_pens[1], large_pens[1], middle - padded[1:-1, 2:]).T
    penalty_down = adaptive(small_pens[2], large_pens[2], middle - padded[:-2, 1:-1])
    penalty_up = adaptive(small_pens[3], large_pens[3], middle - padded[2:, 1:-1])
    disparities = cost_volume.shape[2]
    crossed = jnp.transpose(cost_volume, (1, 0, 2))
    start_rows = jnp.zeros((crossed.shape[1], disparities), jnp.float32)
    start_cols = jnp.zeros((cost_volume.shape[1], disparities), jnp.float32)
    path_right, _ = sweep(crossed, penalty_right, small_pens[0], start_rows, False)
    path_left, _ = sweep(crossed, penalty_left, small_pens[1], start_rows, True)
    across = path_right + path_left
    path_down, _ = sweep(cost_volume, penalty_down, small_pens[2], start_cols, False)
    path_up, _ = sweep(cost_volume, penalty_up, small_pens[3], start_cols, True)
    down_total = path_down + path_up
    return (down_total + jnp.transpose(across, (1, 0, 2))) * OUT_SCALE
```

```python
from functools import partial

import jax
import jax.numpy as jnp
from jax import lax
from jax.experimental import pallas as pl
from jax.experimental.pallas import tpu as pltpu
from jax.sharding import PartitionSpec as P

FAR = 1e30
GRADIENT_GAIN = 4.0
OUT_SCALE = 1.0 / 256.0
LANES = 128
TILES = 32
ROWS = 24


def adaptive(penalty_one, penalty_two, step_diff):
    return penalty_one + (penalty_two - penalty_one) / (1.0 + GRADIENT_GAIN * jnp.abs(step_diff))


def gather_costs(blocks, two, core_ref, sources, scr, img):
    for z in range(blocks // len(sources)):
        for which, source in enumerate(sources):
            if two:
                core = core_ref[0]
                place = 2 * z + core if which == 0 else 2 * z + 1 - core
            else:
                place = z
            scr[place] = source[z, 0:16, :].astype(jnp.bfloat16)
            img[pl.ds(place, 1), :] = source[z, 16:17, 0:LANES]


def path_kernel(blocks, first, two, core_ref, small_ref, large_ref, *refs):
    sources, (out_ref, scr, img, ahead, back, costs, starts, states) = refs[:-8], refs[-8:]
    groups = blocks // 4
    lane = lax.broadcasted_iota(jnp.int32, (8, LANES), 1)
    sub = lax.broadcasted_iota(jnp.int32, (8, LANES), 0)
    gather_costs(blocks, two, core_ref, sources, scr, img)

    place, row = lane[:groups] % 64, sub[:groups]
    line = img[pl.ds(0, groups, stride=4), :]
    for k in range(1, 4):
        line = jnp.where(place // 16 == k, img[pl.ds(k, groups, stride=4), :], line)
    before = pltpu.roll(line, 1, 1)
    wrapped = jnp.concatenate([before[groups - 1 :], before[: groups - 1]], 0)
    before = jnp.where(place == 0, jnp.where(row == 0, 0.0, wrapped), before)
    after = pltpu.roll(line, LANES - 1, 1)
    wrapped = jnp.concatenate([after[1:], after[:1]], 0)
    after = jnp.where(place == 63, jnp.where(row == groups - 1, 0.0, wrapped), after)
    small = [small_ref[first + i].astype(jnp.float32) for i in range(2)]
    large = [large_ref[first + i].astype(jnp.float32) for i in range(2)]
    ahead[...] = adaptive(small[0], large[0], line - before)
    back[...] = adaptive(small[1], large[1], line - after)
    forward = lane < 64
    penalty_one = jnp.where(forward, small[0], small[1])

    to = lax.broadcasted_iota(jnp.int32, (256, 256), 0)
    of = lax.broadcasted_iota(jnp.int32, (256, 256), 1)
    order = (of == (to % 8) * TILES + to // 8).astype(jnp.bfloat16)
    for g in range(groups):
        pixels = jnp.concatenate(
            [
                scr[4 * g : 4 * g + 4].reshape(64, 256),
                scr[blocks - 4 * g - 4 : blocks - 4 * g].reshape(64, 256),
            ],
            0,
        )
        turned = lax.dot_general(
            order, pixels, (((1,), (1,)), ((), ())), preferred_element_type=jnp.float32
        )
        costs[g] = turned.reshape(TILES, 8, LANES)

    def lowest_of(level):
        while len(level) > 1:
            level = [jnp.minimum(level[i], level[i + 1]) for i in range(0, len(level), 2)]
        lowest = level[0]
        for shift in (4, 2, 1):
            lowest = jnp.minimum(lowest, pltpu.roll(lowest, shift, 0))
        return lowest

    def segment(k, path):
        lowest = lowest_of(path)
        path = [x - lowest for x in path]
        here = lane % 64 == k
        for v in range(TILES):
            starts[v] = jnp.where(here, path[v], starts[v])
        g = k // 4
        penalty_two = jnp.where(
            forward,
            jnp.broadcast_to(ahead[pl.ds(g, 1), :], (8, LANES)),
            jnp.broadcast_to(back[pl.ds(groups - 1 - g, 1), :], (8, LANES)),
        )
        base = 16 * (k % 4)
        for j in range(16):
            source = jnp.where(forward, base + j, 127 - base - j)
            jump = jnp.take_along_axis(penalty_two, source, axis=1)
            if j == 0:
                highest = jump
            else:
                highest = lowest_of(path) + jump
            raised = [x + penalty_one for x in path]
            below = jnp.where(sub == 0, FAR, pltpu.roll(raised[-1], 1, 0))
            above = jnp.where(sub == 7, FAR, pltpu.roll(raised[0], 7, 0))
            padded = [below, *raised, above]
            path = [
                jnp.minimum(
                    jnp.minimum(path[v], jnp.minimum(padded[v], padded[v + 2])), highest
                )
                + jnp.take_along_axis(costs[g, v], source, axis=1)
                for v in range(TILES)
            ]
        return tuple(path)

    zero = jnp.zeros((8, LANES), jnp.float32)
    lax.fori_loop(0, blocks, segment, (zero,) * TILES)
    states[...] = jnp.concatenate([starts[:, s, :] for s in range(8)], 0).T
    for z in range(16):
        block = 2 * z + core_ref[0] if two else z
        out_ref[z, 0:1, :] = states[pl.ds(block, 1), :]
        out_ref[z, 1:2, :] = states[pl.ds(64 + blocks - 1 - block, 1), :]
        fore, rear = ahead[pl.ds(block // 4, 1), :], back[pl.ds(block // 4, 1), :]
        out_ref[z, 2:3, :] = jnp.concatenate([fore, fore], 1)
        out_ref[z, 3:4, :] = jnp.concatenate([rear, rear], 1)


def path_states(blocks, first, two, core, p_small, p_large, *sources):
    smem = pl.BlockSpec(memory_space=pltpu.SMEM)
    vmem = pl.BlockSpec(memory_space=pltpu.VMEM)
    return pl.pallas_call(
        partial(path_kernel, blocks, first, two),
        out_shape=jax.ShapeDtypeStruct((16, 4, 256), jnp.float32),
        in_specs=[smem] * 3 + [vmem] * len(sources),
        out_specs=vmem,
        scratch_shapes=[
            pltpu.VMEM((blocks, 16, 256), jnp.bfloat16),
            pltpu.VMEM((blocks, LANES), jnp.float32),
            pltpu.VMEM((blocks // 4, LANES), jnp.float32),
            pltpu.VMEM((blocks // 4, LANES), jnp.float32),
            pltpu.VMEM((blocks // 4, TILES, 8, LANES), jnp.float32),
            pltpu.VMEM((TILES, 8, LANES), jnp.float32),
            pltpu.VMEM((LANES, 256), jnp.float32),
        ],
        compiler_params=pltpu.CompilerParams(vmem_limit_bytes=24 * 2**20),
        cost_estimate=pl.CostEstimate(
            flops=blocks * 16 * 256 * 128 * 8, bytes_accessed=blocks * 24 * 1024, transcendentals=0
        ),
        name="line_paths",
    )(core, p_small, p_large, *sources)


def replay_kernel(first, across, quarter_ref, small_ref, entry_ref, cost_ref, *refs):
    *so_far, out_ref = refs
    lane = lax.broadcasted_iota(jnp.int32, (16, 256), 1)
    shift = (LANES - 16 * quarter_ref[0]) % LANES
    paths = [entry_ref[:, i, :] for i in range(2)]
    jumps = [pltpu.roll(entry_ref[:, 2 + i, 0:LANES], shift, 1) for i in range(2)]
    small = [small_ref[first + i].astype(jnp.float32) for i in range(2)]
    for j in range(16):
        for i, at in enumerate((j, 15 - j)):
            path = paths[i]
            lowest = jnp.min(path, axis=1, keepdims=True)
            below = jnp.where(lane == 0, FAR, pltpu.roll(path, 1, 1))
            above = jnp.where(lane == 255, FAR, pltpu.roll(path, 255, 1))
            chosen = jnp.minimum(path, jnp.minimum(below, above) + small[i])
            chosen = jnp.minimum(chosen, lowest + jumps[i][:, at : at + 1])
            cost = cost_ref[:, at, :] if across else cost_ref[at]
            path = cost.astype(jnp.float32) + chosen - lowest
            paths[i] = path
            here = (slice(None), at) if across else (at,)
            seen = j >= 8
            if across:
                value = path if seen else path + so_far[0][here]
                value = value + out_ref[here] if seen else value
                out_ref[here] = value * OUT_SCALE if seen else value
            else:
                out_ref[here] = path + out_ref[here] if seen else path


def replay(first, across, quarter, p_small, entry, cost, *so_far):
    smem = pl.BlockSpec(memory_space=pltpu.SMEM)
    vmem = pl.BlockSpec(memory_space=pltpu.VMEM)
    return pl.pallas_call(
        partial(replay_kernel, first, across),
        out_shape=jax.ShapeDtypeStruct((16, 16, 256), jnp.float32),
        in_specs=[smem] * 2 + [vmem] * (2 + len(so_far)),
        out_specs=vmem,
        cost_estimate=pl.CostEstimate(
            flops=2 * 65536 * 100, bytes_accessed=2**20, transcendentals=0
        ),
        name="block_paths",
    )(quarter, p_small, entry, cost, *so_far)


def message(cost, image):
    wide = jnp.tile(image, (1, 16))[:, None, :]
    empty = jnp.zeros((16, ROWS - 17, 256), jnp.float32)
    return jnp.concatenate([cost.astype(jnp.float32), wide, empty], 1)


def on_device(cost_volume, left_image, p_small, p_large):
    index_x, index_y = lax.axis_index("gx"), lax.axis_index("gy")
    core = (index_x % 2).reshape(1)
    chips = [[2 * z + c for z in range(16)] for c in range(2)]
    swap = [(i, i ^ 1) for i in range(32)]

    lines = message(cost_volume, left_image)
    lines = lax.all_to_all(lines, "gx", 0, 0, axis_index_groups=chips)
    columns = message(jnp.transpose(cost_volume, (1, 0, 2)), left_image.T)
    columns = lax.all_to_all(columns, "gy", 0, 0)
    others = lax.ppermute(lines, "gx", swap)

    entry_y = path_states(16, 2, False, core, p_small, p_large, columns)
    entry_y = lax.all_to_all(entry_y, "gy", 0, 0)
    entry_x = path_states(32, 0, True, core, p_small, p_large, lines, others)
    entry_x = lax.all_to_all(entry_x, "gx", 0, 0, axis_index_groups=chips)

    total = replay(2, False, (index_y % 4).reshape(1), p_small, entry_y, cost_volume)
    return replay(0, True, (index_x % 4).reshape(1), p_small, entry_x, cost_volume, total)


def solution(mesh):
    in_specs = (P("gy", "gx", None), P("gy", "gx"), P(), P())
    out_specs = P("gy", "gx", None)
    return jax.shard_map(
        on_device, mesh=mesh, in_specs=in_specs, out_specs=out_specs, check_vma=False
    )
```

```python
from functools import partial

import jax
import jax.numpy as jnp
from jax import lax
from jax.experimental import pallas as pl
from jax.experimental.pallas import tpu as pltpu
from jax.sharding import PartitionSpec as P

FAR = 1e30
GRADIENT_GAIN = 4.0
OUT_SCALE = 1.0 / 256.0
LANES = 128
TILES = 32
ROWS = 40


def adaptive(penalty_one, penalty_two, step_diff):
    return penalty_one + (penalty_two - penalty_one) / (1.0 + GRADIENT_GAIN * jnp.abs(step_diff))


def gather_costs(blocks, two, core_ref, sources, scr, img):
    for z in range(blocks // len(sources)):
        for which, source in enumerate(sources):
            if two:
                core = core_ref[0]
                place = 2 * z + core if which == 0 else 2 * z + 1 - core
            else:
                place = z
            scr[place, :, 0:LANES] = source[z, 0:16, :].astype(jnp.bfloat16)
            scr[place, :, LANES:] = source[z, 16:32, :].astype(jnp.bfloat16)
            img[pl.ds(place, 1), :] = source[z, 32:33, :]


def path_kernel(blocks, first, two, core_ref, small_ref, large_ref, *refs):
    sources, (out_ref, scr, img, ahead, back, costs, starts, states) = refs[:-8], refs[-8:]
    groups = blocks // 4
    lane = lax.broadcasted_iota(jnp.int32, (8, LANES), 1)
    sub = lax.broadcasted_iota(jnp.int32, (8, LANES), 0)
    gather_costs(blocks, two, core_ref, sources, scr, img)

    place, row = lane[:groups] % 64, sub[:groups]
    line = img[pl.ds(0, groups, stride=4), :]
    for k in range(1, 4):
        line = jnp.where(place // 16 == k, img[pl.ds(k, groups, stride=4), :], line)
    before = pltpu.roll(line, 1, 1)
    wrapped = jnp.concatenate([before[groups - 1 :], before[: groups - 1]], 0)
    before = jnp.where(place == 0, jnp.where(row == 0, 0.0, wrapped), before)
    after = pltpu.roll(line, LANES - 1, 1)
    wrapped = jnp.concatenate([after[1:], after[:1]], 0)
    after = jnp.where(place == 63, jnp.where(row == groups - 1, 0.0, wrapped), after)
    small = [small_ref[first + i].astype(jnp.float32) for i in range(2)]
    large = [large_ref[first + i].astype(jnp.float32) for i in range(2)]
    ahead[...] = adaptive(small[0], large[0], line - before)
    back[...] = adaptive(small[1], large[1], line - after)
    forward = lane < 64
    penalty_one = jnp.where(forward, small[0], small[1])

    to = lax.broadcasted_iota(jnp.int32, (256, 256), 0)
    of = lax.broadcasted_iota(jnp.int32, (256, 256), 1)
    order = (of == (to % 8) * TILES + to // 8).astype(jnp.bfloat16)
    for g in range(groups):
        pixels = jnp.concatenate(
            [
                scr[4 * g : 4 * g + 4].reshape(64, 256),
                scr[blocks - 4 * g - 4 : blocks - 4 * g].reshape(64, 256),
            ],
            0,
        )
        turned = lax.dot_general(
            order, pixels, (((1,), (1,)), ((), ())), preferred_element_type=jnp.float32
        )
        costs[g] = turned.reshape(TILES, 8, LANES)

    def lowest_of(level):
        while len(level) > 1:
            level = [jnp.minimum(level[i], level[i + 1]) for i in range(0, len(level), 2)]
        lowest = level[0]
        for shift in (4, 2, 1):
            lowest = jnp.minimum(lowest, pltpu.roll(lowest, shift, 0))
        return lowest

    def segment(k, path):
        lowest = lowest_of(path)
        path = [x - lowest for x in path]
        here = lane % 64 == k
        for v in range(TILES):
            starts[v] = jnp.where(here, path[v], starts[v])
        g = k // 4
        penalty_two = jnp.where(
            forward,
            jnp.broadcast_to(ahead[pl.ds(g, 1), :], (8, LANES)),
            jnp.broadcast_to(back[pl.ds(groups - 1 - g, 1), :], (8, LANES)),
        )
        base = 16 * (k % 4)
        for j in range(16):
            source = jnp.where(forward, base + j, 127 - base - j)
            jump = jnp.take_along_axis(penalty_two, source, axis=1)
            if j == 0:
                highest = jump
            else:
                highest = lowest_of(path) + jump
            raised = [x + penalty_one for x in path]
            below = jnp.where(sub == 0, FAR, pltpu.roll(raised[-1], 1, 0))
            above = jnp.where(sub == 7, FAR, pltpu.roll(raised[0], 7, 0))
            padded = [below, *raised, above]
            path = [
                jnp.minimum(
                    jnp.minimum(path[v], jnp.minimum(padded[v], padded[v + 2])), highest
                )
                + jnp.take_along_axis(costs[g, v], source, axis=1)
                for v in range(TILES)
            ]
        return tuple(path)

    zero = jnp.zeros((8, LANES), jnp.float32)
    lax.fori_loop(0, blocks, segment, (zero,) * TILES)
    states[...] = jnp.concatenate([starts[:, s, :] for s in range(8)], 0).T
    for z in range(16):
        block = 2 * z + core_ref[0] if two else z
        out_ref[z, 0:1, :] = states[pl.ds(block, 1), :]
        out_ref[z, 1:2, :] = states[pl.ds(64 + blocks - 1 - block, 1), :]
        fore, rear = ahead[pl.ds(block // 4, 1), :], back[pl.ds(block // 4, 1), :]
        out_ref[z, 2:3, :] = jnp.concatenate([fore, fore], 1)
        out_ref[z, 3:4, :] = jnp.concatenate([rear, rear], 1)


def path_states(blocks, first, two, core, p_small, p_large, *sources):
    smem = pl.BlockSpec(memory_space=pltpu.SMEM)
    vmem = pl.BlockSpec(memory_space=pltpu.VMEM)
    return pl.pallas_call(
        partial(path_kernel, blocks, first, two),
        out_shape=jax.ShapeDtypeStruct((16, 4, 256), jnp.float32),
        in_specs=[smem] * 3 + [vmem] * len(sources),
        out_specs=vmem,
        scratch_shapes=[
            pltpu.VMEM((blocks, 16, 256), jnp.bfloat16),
            pltpu.VMEM((blocks, LANES), jnp.float32),
            pltpu.VMEM((blocks // 4, LANES), jnp.float32),
            pltpu.VMEM((blocks // 4, LANES), jnp.float32),
            pltpu.VMEM((blocks // 4, TILES, 8, LANES), jnp.float32),
            pltpu.VMEM((TILES, 8, LANES), jnp.float32),
            pltpu.VMEM((LANES, 256), jnp.float32),
        ],
        compiler_params=pltpu.CompilerParams(vmem_limit_bytes=24 * 2**20),
        cost_estimate=pl.CostEstimate(
            flops=blocks * 16 * 256 * 128 * 8, bytes_accessed=blocks * 24 * 1024, transcendentals=0
        ),
        name="line_paths",
    )(core, p_small, p_large, *sources)


def replay_kernel(first, across, quarter_ref, small_ref, entry_ref, cost_ref, *refs):
    *so_far, out_ref = refs
    lane = lax.broadcasted_iota(jnp.int32, (16, 256), 1)
    shift = (LANES - 16 * quarter_ref[0]) % LANES
    paths = [entry_ref[:, i, :] for i in range(2)]
    jumps = [pltpu.roll(entry_ref[:, 2 + i, 0:LANES], shift, 1) for i in range(2)]
    small = [small_ref[first + i].astype(jnp.float32) for i in range(2)]
    for j in range(16):
        for i, at in enumerate((j, 15 - j)):
            path = paths[i]
            lowest = jnp.min(path, axis=1, keepdims=True)
            below = jnp.where(lane == 0, FAR, pltpu.roll(path, 1, 1))
            above = jnp.where(lane == 255, FAR, pltpu.roll(path, 255, 1))
            chosen = jnp.minimum(path, jnp.minimum(below, above) + small[i])
            chosen = jnp.minimum(chosen, lowest + jumps[i][:, at : at + 1])
            cost = cost_ref[:, at, :] if across else cost_ref[at]
            path = cost.astype(jnp.float32) + chosen - lowest
            paths[i] = path
            here = (slice(None), at) if across else (at,)
            seen = j >= 8
            if across:
                value = path if seen else path + so_far[0][here]
                value = value + out_ref[here] if seen else value
                out_ref[here] = value * OUT_SCALE if seen else value
            else:
                out_ref[here] = path + out_ref[here] if seen else path


def replay(first, across, quarter, p_small, entry, cost, *so_far):
    smem = pl.BlockSpec(memory_space=pltpu.SMEM)
    vmem = pl.BlockSpec(memory_space=pltpu.VMEM)
    return pl.pallas_call(
        partial(replay_kernel, first, across),
        out_shape=jax.ShapeDtypeStruct((16, 16, 256), jnp.float32),
        in_specs=[smem] * 2 + [vmem] * (2 + len(so_far)),
        out_specs=vmem,
        cost_estimate=pl.CostEstimate(
            flops=2 * 65536 * 100, bytes_accessed=2**20, transcendentals=0
        ),
        name="block_paths",
    )(quarter, p_small, entry, cost, *so_far)


def message(cost, image):
    wide = jnp.tile(image, (1, LANES // 16))[:, None, :]
    empty = jnp.zeros((16, ROWS - 33, LANES), jnp.float32)
    cost = cost.astype(jnp.float32)
    return jnp.concatenate([cost[:, :, :LANES], cost[:, :, LANES:], wide, empty], 1)


def after_kernel(value_ref, earlier_ref, out_ref):
    pass


def after(value, earlier):
    anywhere = pl.BlockSpec(memory_space=pl.ANY)
    return pl.pallas_call(
        after_kernel,
        out_shape=jax.ShapeDtypeStruct(value.shape, value.dtype),
        in_specs=[anywhere] * 2,
        out_specs=anywhere,
        input_output_aliases={0: 0},
        name="after",
    )(value, earlier)


def on_device(cost_volume, left_image, p_small, p_large):
    index_x, index_y = lax.axis_index("gx"), lax.axis_index("gy")
    core = (index_x % 2).reshape(1)
    chips = [[2 * z + c for z in range(16)] for c in range(2)]
    swap = [(i, i ^ 1) for i in range(32)]

    columns = message(jnp.transpose(cost_volume, (1, 0, 2)), left_image.T)
    lines = message(cost_volume, left_image)
    columns = lax.all_to_all(columns, "gy", 0, 0)
    lines = after(lines, columns[:1, :8])
    lines = lax.all_to_all(lines, "gx", 0, 0, axis_index_groups=chips)
    entry_y = path_states(16, 2, False, core, p_small, p_large, columns)
    lines = after(lines, entry_y)
    others = lax.ppermute(lines, "gx", swap)

    entry_y = lax.all_to_all(entry_y, "gy", 0, 0)
    entry_x = path_states(32, 0, True, core, p_small, p_large, lines, others)
    entry_x = lax.all_to_all(entry_x, "gx", 0, 0, axis_index_groups=chips)

    total = replay(2, False, (index_y % 4).reshape(1), p_small, entry_y, cost_volume)
    return replay(0, True, (index_x % 4).reshape(1), p_small, entry_x, cost_volume, total)


def solution(mesh):
    in_specs = (P("gy", "gx", None), P("gy", "gx"), P(), P())
    out_specs = P("gy", "gx", None)
    return jax.shard_map(
        on_device, mesh=mesh, in_specs=in_specs, out_specs=out_specs, check_vma=False
    )
```

```python
from functools import partial

import jax
import jax.numpy as jnp
from jax import lax
from jax.experimental import pallas as pl
from jax.experimental.pallas import tpu as pltpu
from jax.sharding import PartitionSpec as P

FAR = 1e30
GRADIENT_GAIN = 4.0
OUT_SCALE = 1.0 / 256.0
LANES = 128
TILES = 32
ROWS = 40


def adaptive(penalty_one, penalty_two, step_diff):
    return penalty_one + (penalty_two - penalty_one) / (1.0 + GRADIENT_GAIN * jnp.abs(step_diff))


def gather_costs(blocks, two, core_ref, sources, scr, img):
    for z in range(blocks // len(sources)):
        for which, source in enumerate(sources):
            if two:
                core = core_ref[0]
                place = 2 * z + core if which == 0 else 2 * z + 1 - core
            else:
                place = z
            scr[place, :, 0:LANES] = source[z, 0:16, :].astype(jnp.bfloat16)
            scr[place, :, LANES:] = source[z, 16:32, :].astype(jnp.bfloat16)
            img[pl.ds(place, 1), :] = source[z, 32:33, :]


def path_kernel(blocks, first, two, core_ref, small_ref, large_ref, *refs):
    sources, (out_ref, scr, img, ahead, back, costs, pick, starts, states) = refs[:-9], refs[-9:]
    groups = blocks // 4
    lane = lax.broadcasted_iota(jnp.int32, (8, LANES), 1)
    sub = lax.broadcasted_iota(jnp.int32, (8, LANES), 0)
    gather_costs(blocks, two, core_ref, sources, scr, img)

    place, row = lane[:groups] % 64, sub[:groups]
    line = img[pl.ds(0, groups, stride=4), :]
    for k in range(1, 4):
        line = jnp.where(place // 16 == k, img[pl.ds(k, groups, stride=4), :], line)
    before = pltpu.roll(line, 1, 1)
    wrapped = jnp.concatenate([before[groups - 1 :], before[: groups - 1]], 0)
    before = jnp.where(place == 0, jnp.where(row == 0, 0.0, wrapped), before)
    after = pltpu.roll(line, LANES - 1, 1)
    wrapped = jnp.concatenate([after[1:], after[:1]], 0)
    after = jnp.where(place == 63, jnp.where(row == groups - 1, 0.0, wrapped), after)
    small = [small_ref[first + i].astype(jnp.float32) for i in range(2)]
    large = [large_ref[first + i].astype(jnp.float32) for i in range(2)]
    ahead[...] = adaptive(small[0], large[0], line - before)
    back[...] = adaptive(small[1], large[1], line - after)
    forward = lane < 64
    penalty_one = jnp.where(forward, small[0], small[1])

    to = lax.broadcasted_iota(jnp.int32, (256, 256), 0)
    of = lax.broadcasted_iota(jnp.int32, (256, 256), 1)
    order = (of == (to % 8) * TILES + to // 8).astype(jnp.bfloat16)
    for g in range(groups):
        pixels = jnp.concatenate(
            [
                scr[4 * g : 4 * g + 4].reshape(64, 256),
                scr[blocks - 4 * g - 4 : blocks - 4 * g].reshape(64, 256),
            ],
            0,
        )
        turned = lax.dot_general(
            order, pixels, (((1,), (1,)), ((), ())), preferred_element_type=jnp.float32
        )
        costs[g] = turned.astype(jnp.bfloat16)

    mirror = jnp.where(lane < 64, 0, LANES - 1)
    lane_in = lax.broadcasted_iota(jnp.int32, (LANES, LANES), 0)
    lane_out = lax.broadcasted_iota(jnp.int32, (LANES, LANES), 1)

    def build(i, nothing):
        pick[i] = (lane_in == jnp.where(lane_out < 64, i, LANES - 1 - i)).astype(jnp.bfloat16)
        return nothing

    lax.fori_loop(0, 64, build, 0)

    def across_sublanes(lowest):
        for shift in (4, 2, 1):
            lowest = jnp.minimum(lowest, pltpu.roll(lowest, shift, 0))
        return lowest

    def halved(level):
        return [jnp.minimum(level[i], level[i + 1]) for i in range(0, len(level), 2)]

    def lowest_of(level):
        while len(level) > 1:
            level = halved(level)
        return across_sublanes(level[0])

    def segments(t, path):
        path = list(path)
        g = t // 2
        base = 32 * (t % 2)
        penalty_two = jnp.where(
            forward,
            jnp.broadcast_to(ahead[pl.ds(g, 1), :], (8, LANES)),
            jnp.broadcast_to(back[pl.ds(groups - 1 - g, 1), :], (8, LANES)),
        )
        lowest = lowest_of(path)
        ordered = penalty_one
        for i in range(32):
            if i % 16 == 0:
                path = [x - lowest for x in path]
                lowest = jnp.zeros_like(lowest)
                here = lane % 64 == 2 * t + i // 16
                for v in range(TILES):
                    starts[v] = jnp.where(here, path[v], starts[v])
            highest = lowest + jnp.take_along_axis(penalty_two, mirror ^ (base + i), axis=1)
            cost = jnp.dot(costs[g], pick[base + i], preferred_element_type=jnp.float32)
            cost = cost.reshape(TILES, 8, LANES)
            raised = [x + ordered for x in path]
            below = jnp.where(sub == 0, FAR, pltpu.roll(raised[-1], 1, 0))
            above = jnp.where(sub == 7, FAR, pltpu.roll(raised[0], 7, 0))
            padded = [below, *raised, above]
            near = [
                jnp.minimum(path[v], jnp.minimum(padded[v], padded[v + 2])) for v in range(TILES)
            ]
            path = [jnp.minimum(near[v], highest) + cost[v] for v in range(TILES)]
            pairs = halved(path)
            ordered = jnp.maximum(penalty_one, jnp.minimum(pairs[-1], -FAR))
            lowest = lowest_of(pairs)
        return tuple(path)

    zero = jnp.zeros((8, LANES), jnp.float32)
    lax.fori_loop(0, blocks // 2, segments, (zero,) * TILES)
    states[...] = jnp.concatenate([starts[:, s, :] for s in range(8)], 0).T
    for z in range(16):
        block = 2 * z + core_ref[0] if two else z
        fore, rear = ahead[pl.ds(block // 4, 1), :], back[pl.ds(block // 4, 1), :]
        start, end = states[pl.ds(block, 1), :], states[pl.ds(64 + blocks - 1 - block, 1), :]
        if two:
            out_ref[z, 0:1, :] = jnp.concatenate([start, fore], 1)
            out_ref[z, 1:2, :] = jnp.concatenate([end, rear], 1)
        else:
            out_ref[2 * z : 2 * z + 1, :] = jnp.concatenate([start, fore, fore], 1)
            out_ref[2 * z + 1 : 2 * z + 2, :] = jnp.concatenate([end, rear, rear], 1)


def path_states(blocks, first, two, core, p_small, p_large, *sources):
    smem = pl.BlockSpec(memory_space=pltpu.SMEM)
    vmem = pl.BlockSpec(memory_space=pltpu.VMEM)
    return pl.pallas_call(
        partial(path_kernel, blocks, first, two),
        out_shape=jax.ShapeDtypeStruct((16, 2, 384) if two else (32, 512), jnp.float32),
        in_specs=[smem] * 3 + [vmem] * len(sources),
        out_specs=vmem,
        scratch_shapes=[
            pltpu.VMEM((blocks, 16, 256), jnp.bfloat16),
            pltpu.VMEM((blocks, LANES), jnp.float32),
            pltpu.VMEM((blocks // 4, LANES), jnp.float32),
            pltpu.VMEM((blocks // 4, LANES), jnp.float32),
            pltpu.VMEM((blocks // 4, 256, LANES), jnp.bfloat16),
            pltpu.VMEM((64, LANES, LANES), jnp.bfloat16),
            pltpu.VMEM((TILES, 8, LANES), jnp.float32),
            pltpu.VMEM((LANES, 256), jnp.float32),
        ],
        compiler_params=pltpu.CompilerParams(vmem_limit_bytes=24 * 2**20),
        cost_estimate=pl.CostEstimate(
            flops=blocks * 16 * 256 * 128 * 8, bytes_accessed=blocks * 24 * 1024, transcendentals=0
        ),
        name="line_paths",
    )(core, p_small, p_large, *sources)


def replay_kernel(first, across, quarter_ref, small_ref, entry_ref, cost_ref, *refs):
    *so_far, out_ref = refs
    lane = lax.broadcasted_iota(jnp.int32, (16, 256), 1)
    shift = (LANES - 16 * quarter_ref[0]) % LANES
    paths = [entry_ref[:, i, 0:256] for i in range(2)]
    jumps = [pltpu.roll(entry_ref[:, i, 256:], shift, 1) for i in range(2)]
    small = [small_ref[first + i].astype(jnp.float32) for i in range(2)]
    lowest = [jnp.min(path, axis=1, keepdims=True) for path in paths]
    for j in range(16):
        for i, at in enumerate((j, 15 - j)):
            path = paths[i]
            cost = (cost_ref[:, at, :] if across else cost_ref[at]).astype(jnp.float32)
            below = jnp.where(lane == 0, FAR, pltpu.roll(path, 1, 1))
            above = jnp.where(lane == 255, FAR, pltpu.roll(path, 255, 1))
            near = jnp.minimum(path, jnp.minimum(below, above) + small[i]) + cost
            highest = lowest[i] + jumps[i][:, at : at + 1]
            path = jnp.minimum(near, highest + cost)
            value = path - lowest[i]
            lowest[i] = jnp.minimum(
                jnp.min(near, axis=1, keepdims=True),
                highest + jnp.min(cost, axis=1, keepdims=True),
            )
            paths[i] = path
            here = (slice(None), at) if across else (at,)
            seen = j >= 8
            if seen:
                value = value + out_ref[here]
            elif across:
                value = value + so_far[0][here]
            out_ref[here] = value * OUT_SCALE if across and seen else value


def replay(first, across, quarter, p_small, entry, cost, *so_far):
    smem = pl.BlockSpec(memory_space=pltpu.SMEM)
    vmem = pl.BlockSpec(memory_space=pltpu.VMEM)
    return pl.pallas_call(
        partial(replay_kernel, first, across),
        out_shape=jax.ShapeDtypeStruct((16, 16, 256), jnp.float32),
        in_specs=[smem] * 2 + [vmem] * (2 + len(so_far)),
        out_specs=vmem,
        cost_estimate=pl.CostEstimate(
            flops=2 * 65536 * 100, bytes_accessed=2**20, transcendentals=0
        ),
        name="block_paths",
    )(quarter, p_small, entry, cost, *so_far)


def message(cost, image):
    wide = jnp.tile(image, (1, LANES // 16))[:, None, :]
    empty = jnp.zeros((16, ROWS - 33, LANES), jnp.float32)
    cost = cost.astype(jnp.float32)
    return jnp.concatenate([cost[:, :, :LANES], cost[:, :, LANES:], wide, empty], 1)


def together_kernel(*refs):
    pass


def together(first, second):
    anywhere = pl.BlockSpec(memory_space=pl.ANY)
    return pl.pallas_call(
        together_kernel,
        out_shape=[jax.ShapeDtypeStruct(x.shape, x.dtype) for x in (first, second)],
        in_specs=[anywhere] * 2,
        out_specs=[anywhere] * 2,
        input_output_aliases={0: 0, 1: 1},
        name="together",
    )(first, second)


def on_device(cost_volume, left_image, p_small, p_large):
    index_x, index_y = lax.axis_index("gx"), lax.axis_index("gy")
    core = (index_x % 2).reshape(1)
    chips = [[2 * z + c for z in range(16)] for c in range(2)]
    swap = [(i, i ^ 1) for i in range(32)]

    columns = message(jnp.transpose(cost_volume, (1, 0, 2)), left_image.T)
    lines = message(cost_volume, left_image)
    columns = lax.all_to_all(columns, "gy", 0, 0)
    lines, columns = together(lines, columns)
    lines = lax.all_to_all(lines, "gx", 0, 0, axis_index_groups=chips)
    entry_y = path_states(16, 2, False, core, p_small, p_large, columns)
    lines, entry_y = together(lines, entry_y)
    others = lax.ppermute(lines, "gx", swap)

    entry_y = lax.all_gather(entry_y, "gy", axis=0, tiled=True).reshape(16, 32, 512)
    entry_y = lax.dynamic_slice(entry_y, (0, 2 * index_y, 0), (16, 2, 384))
    entry_x = path_states(32, 0, True, core, p_small, p_large, lines, others)
    entry_x = lax.all_to_all(entry_x, "gx", 0, 0, axis_index_groups=chips)

    total = replay(2, False, (index_y % 4).reshape(1), p_small, entry_y, cost_volume)
    return replay(0, True, (index_x % 4).reshape(1), p_small, entry_x, cost_volume, total)


def solution(mesh):
    in_specs = (P("gy", "gx", None), P("gy", "gx"), P(), P())
    out_specs = P("gy", "gx", None)
    return jax.shard_map(
        on_device, mesh=mesh, in_specs=in_specs, out_specs=out_specs, check_vma=False
    )
```

```python
from functools import partial

import jax
import jax.numpy as jnp
from jax import lax
from jax.experimental import pallas as pl
from jax.experimental.pallas import tpu as pltpu
from jax.sharding import PartitionSpec as P

FAR = 1e30
GRADIENT_GAIN = 4.0
OUT_SCALE = 1.0 / 256.0
LANES = 128
TILES = 32
ROWS = 40


def adaptive(penalty_one, penalty_two, step_diff):
    return penalty_one + (penalty_two - penalty_one) / (1.0 + GRADIENT_GAIN * jnp.abs(step_diff))


def gather_costs(blocks, two, core, sources, scr, img):
    for z in range(blocks // len(sources)):
        for which, source in enumerate(sources):
            if two:
                place = 2 * z + core if which == 0 else 2 * z + 1 - core
            else:
                place = z
            scr[place, :, 0:LANES] = source[z, 0:16, :].astype(jnp.bfloat16)
            scr[place, :, LANES:] = source[z, 16:32, :].astype(jnp.bfloat16)
            img[pl.ds(place, 1), :] = source[z, 32:33, :]


def path_kernel(blocks, first, two, numbers_ref, *refs):
    sources, (out_ref, scr, img, ahead, back, costs, pick, ready, starts, states) = refs[:-10], refs[-10:]
    groups = blocks // 4
    lane = lax.broadcasted_iota(jnp.int32, (8, LANES), 1)
    sub = lax.broadcasted_iota(jnp.int32, (8, LANES), 0)
    gather_costs(blocks, two, numbers_ref[8], sources, scr, img)

    place, row = lane[:groups] % 64, sub[:groups]
    line = img[pl.ds(0, groups, stride=4), :]
    for k in range(1, 4):
        line = jnp.where(place // 16 == k, img[pl.ds(k, groups, stride=4), :], line)
    before = pltpu.roll(line, 1, 1)
    wrapped = jnp.concatenate([before[groups - 1 :], before[: groups - 1]], 0)
    before = jnp.where(place == 0, jnp.where(row == 0, 0.0, wrapped), before)
    after = pltpu.roll(line, LANES - 1, 1)
    wrapped = jnp.concatenate([after[1:], after[:1]], 0)
    after = jnp.where(place == 63, jnp.where(row == groups - 1, 0.0, wrapped), after)
    small = [numbers_ref[first + i].astype(jnp.float32) for i in range(2)]
    large = [numbers_ref[4 + first + i].astype(jnp.float32) for i in range(2)]
    ahead[...] = adaptive(small[0], large[0], line - before)
    back[...] = adaptive(small[1], large[1], line - after)
    forward = lane < 64
    penalty_one = jnp.where(forward, small[0], small[1])

    to = lax.broadcasted_iota(jnp.int32, (256, 256), 0)
    of = lax.broadcasted_iota(jnp.int32, (256, 256), 1)
    order = (of == (to % 8) * TILES + to // 8).astype(jnp.bfloat16)
    for g in range(groups):
        pixels = jnp.concatenate(
            [
                scr[4 * g : 4 * g + 4].reshape(64, 256),
                scr[blocks - 4 * g - 4 : blocks - 4 * g].reshape(64, 256),
            ],
            0,
        )
        turned = lax.dot_general(
            order, pixels, (((1,), (1,)), ((), ())), preferred_element_type=jnp.float32
        )
        costs[g] = turned.astype(jnp.bfloat16)

    mirror = jnp.where(lane < 64, 0, LANES - 1)
    lane_in = lax.broadcasted_iota(jnp.int32, (LANES, LANES), 0)
    lane_out = lax.broadcasted_iota(jnp.int32, (LANES, LANES), 1)

    def build(i, nothing):
        pick[i] = (lane_in == jnp.where(lane_out < 64, i, LANES - 1 - i)).astype(jnp.bfloat16)
        return nothing

    lax.fori_loop(0, 64, build, 0)

    def across_sublanes(lowest):
        for shift in (4, 2, 1):
            lowest = jnp.minimum(lowest, pltpu.roll(lowest, shift, 0))
        return lowest

    def halved(level):
        return [jnp.minimum(level[i], level[i + 1]) for i in range(0, len(level), 2)]

    def lowest_of(level):
        while len(level) > 1:
            level = halved(level)
        return across_sublanes(level[0])

    def costs_at(g, i):
        cost = jnp.dot(costs[g], pick[i], preferred_element_type=jnp.float32)
        return cost.reshape(TILES, 8, LANES)

    ready[...] = costs_at(0, 0)

    def segments(t, path):
        path = list(path)
        g = t // 2
        base = 32 * (t % 2)
        penalty_two = jnp.where(
            forward,
            jnp.broadcast_to(ahead[pl.ds(g, 1), :], (8, LANES)),
            jnp.broadcast_to(back[pl.ds(groups - 1 - g, 1), :], (8, LANES)),
        )
        lowest = lowest_of(path)
        ordered = penalty_one
        for i in range(32):
            if i % 16 == 0:
                path = [x - lowest for x in path]
                lowest = jnp.zeros_like(lowest)
                here = lane % 64 == 2 * t + i // 16
                for v in range(TILES):
                    starts[v] = jnp.where(here, path[v], starts[v])
            highest = lowest + jnp.take_along_axis(penalty_two, mirror ^ (base + i), axis=1)
            cost = ready if i == 0 else costs_at(g, base + i)
            raised = [x + ordered for x in path]
            below = jnp.where(sub == 0, FAR, pltpu.roll(raised[-1], 1, 0))
            above = jnp.where(sub == 7, FAR, pltpu.roll(raised[0], 7, 0))
            padded = [below, *raised, above]
            near = [
                jnp.minimum(path[v], jnp.minimum(padded[v], padded[v + 2])) for v in range(TILES)
            ]
            path = [jnp.minimum(near[v], highest) + cost[v] for v in range(TILES)]
            pairs = halved(path)
            ordered = jnp.maximum(penalty_one, jnp.minimum(pairs[-1], -FAR))
            lowest = lowest_of(pairs)
            if i == 28:
                later = jnp.minimum(t + 1, blocks // 2 - 1)
                ready[...] = costs_at(later // 2, 32 * (later % 2))
        return tuple(path)

    zero = jnp.zeros((8, LANES), jnp.float32)
    lax.fori_loop(0, blocks // 2, segments, (zero,) * TILES)
    states[...] = jnp.concatenate([starts[:, s, :] for s in range(8)], 0).T
    for z in range(16):
        block = 2 * z + numbers_ref[8] if two else z
        fore, rear = ahead[pl.ds(block // 4, 1), :], back[pl.ds(block // 4, 1), :]
        start, end = states[pl.ds(block, 1), :], states[pl.ds(64 + blocks - 1 - block, 1), :]
        out_ref[z, 0:1, :] = jnp.concatenate([start, fore], 1)
        out_ref[z, 1:2, :] = jnp.concatenate([end, rear], 1)


def path_states(blocks, first, two, numbers, *sources):
    smem = pl.BlockSpec(memory_space=pltpu.SMEM)
    vmem = pl.BlockSpec(memory_space=pltpu.VMEM)
    return pl.pallas_call(
        partial(path_kernel, blocks, first, two),
        out_shape=jax.ShapeDtypeStruct((16, 2, 384), jnp.float32),
        in_specs=[smem] + [vmem] * len(sources),
        out_specs=vmem,
        scratch_shapes=[
            pltpu.VMEM((blocks, 16, 256), jnp.bfloat16),
            pltpu.VMEM((blocks, LANES), jnp.float32),
            pltpu.VMEM((blocks // 4, LANES), jnp.float32),
            pltpu.VMEM((blocks // 4, LANES), jnp.float32),
            pltpu.VMEM((blocks // 4, 256, LANES), jnp.bfloat16),
            pltpu.VMEM((64, LANES, LANES), jnp.bfloat16),
            pltpu.VMEM((TILES, 8, LANES), jnp.float32),
            pltpu.VMEM((TILES, 8, LANES), jnp.float32),
            pltpu.VMEM((LANES, 256), jnp.float32),
        ],
        compiler_params=pltpu.CompilerParams(vmem_limit_bytes=12 * 2**20),
        cost_estimate=pl.CostEstimate(
            flops=blocks * 16 * 256 * 128 * 8, bytes_accessed=blocks * 24 * 1024, transcendentals=0
        ),
        name="line_paths",
    )(numbers, *sources)


def replay_kernel(first, across, numbers_ref, entry_ref, cost_ref, *refs):
    *so_far, out_ref = refs
    lane = lax.broadcasted_iota(jnp.int32, (16, 256), 1)
    shift = (LANES - 16 * numbers_ref[9 if across else 10]) % LANES
    paths = [entry_ref[:, i, 0:256] for i in range(2)]
    jumps = [pltpu.roll(entry_ref[:, i, 256:], shift, 1) for i in range(2)]
    small = [numbers_ref[first + i].astype(jnp.float32) for i in range(2)]
    lowest = [jnp.min(path, axis=1, keepdims=True) for path in paths]
    for j in range(16):
        for i, at in enumerate((j, 15 - j)):
            path = paths[i]
            cost = (cost_ref[:, at, :] if across else cost_ref[at]).astype(jnp.float32)
            below = jnp.where(lane == 0, FAR, pltpu.roll(path, 1, 1))
            above = jnp.where(lane == 255, FAR, pltpu.roll(path, 255, 1))
            near = jnp.minimum(path, jnp.minimum(below, above) + small[i]) + cost
            highest = lowest[i] + jumps[i][:, at : at + 1]
            path = jnp.minimum(near, highest + cost)
            value = path - lowest[i]
            lowest[i] = jnp.minimum(
                jnp.min(near, axis=1, keepdims=True),
                highest + jnp.min(cost, axis=1, keepdims=True),
            )
            paths[i] = path
            here = (slice(None), at) if across else (at,)
            seen = j >= 8
            if seen:
                value = value + out_ref[here]
            elif across:
                value = value + so_far[0][here]
            out_ref[here] = value * OUT_SCALE if across and seen else value


def replay(first, across, numbers, entry, cost, *so_far):
    smem = pl.BlockSpec(memory_space=pltpu.SMEM)
    vmem = pl.BlockSpec(memory_space=pltpu.VMEM)
    return pl.pallas_call(
        partial(replay_kernel, first, across),
        out_shape=jax.ShapeDtypeStruct((16, 16, 256), jnp.float32),
        in_specs=[smem] + [vmem] * (2 + len(so_far)),
        out_specs=vmem,
        cost_estimate=pl.CostEstimate(
            flops=2 * 65536 * 100, bytes_accessed=2**20, transcendentals=0
        ),
        compiler_params=pltpu.CompilerParams(vmem_limit_bytes=3 * 2**20),
        name="block_paths",
    )(numbers, entry, cost, *so_far)


def message(cost, image):
    wide = jnp.tile(image, (1, LANES // 16))[:, None, :]
    empty = jnp.zeros((16, ROWS - 33, LANES), jnp.float32)
    cost = cost.astype(jnp.float32)
    return jnp.concatenate([cost[:, :, :LANES], cost[:, :, LANES:], wide, empty], 1)


def after_kernel(value_ref, earlier_ref, out_ref):
    out_ref[...] = value_ref[...]


def after(value, earlier):
    vmem = pl.BlockSpec(memory_space=pltpu.VMEM)
    return pl.pallas_call(
        after_kernel,
        out_shape=jax.ShapeDtypeStruct(value.shape, value.dtype),
        in_specs=[vmem] * 2,
        out_specs=vmem,
        compiler_params=pltpu.CompilerParams(vmem_limit_bytes=2 * 2**20),
        name="after",
    )(value, earlier)


def on_device(cost_volume, left_image, p_small, p_large):
    index_x, index_y = lax.axis_index("gx"), lax.axis_index("gy")
    here = jnp.stack([index_x % 2, index_x % 4, index_y % 4]).astype(jnp.int32)
    numbers = jnp.concatenate([p_small, p_large, here])
    chips = [[2 * z + c for z in range(16)] for c in range(2)]
    swap = [(i, i ^ 1) for i in range(32)]

    columns = message(jnp.transpose(cost_volume, (1, 0, 2)), left_image.T)
    lines = message(cost_volume, left_image)
    columns = lax.all_to_all(columns, "gy", 0, 0)
    lines = after(lines, columns)
    lines = lax.all_to_all(lines, "gx", 0, 0, axis_index_groups=chips)
    entry_y = path_states(16, 2, False, numbers, columns)
    lines = after(lines, entry_y)
    others = lax.ppermute(lines, "gx", swap)

    entry_y = lax.all_to_all(entry_y, "gy", 0, 0)
    entry_x = path_states(32, 0, True, numbers, lines, others)
    entry_x = lax.all_to_all(entry_x, "gx", 0, 0, axis_index_groups=chips)

    total = replay(2, False, numbers, entry_y, cost_volume)
    return replay(0, True, numbers, entry_x, cost_volume, total)


def solution(mesh):
    in_specs = (P("gy", "gx", None), P("gy", "gx"), P(), P())
    out_specs = P("gy", "gx", None)
    return jax.shard_map(
        on_device, mesh=mesh, in_specs=in_specs, out_specs=out_specs, check_vma=False
    )
```

```python
from functools import partial

import jax
import jax.numpy as jnp
from jax import lax
from jax.experimental import pallas as pl
from jax.experimental.pallas import tpu as pltpu
from jax.sharding import PartitionSpec as P

FAR = 1e30
GRADIENT_GAIN = 4.0
OUT_SCALE = 1.0 / 256.0
LANES = 128
TILES = 32
UNROLL = 4
AHEAD = 3
ROWS = 40


def adaptive(penalty_one, penalty_two, step_diff):
    return penalty_one + (penalty_two - penalty_one) / (1.0 + GRADIENT_GAIN * jnp.abs(step_diff))


def gather_costs(blocks, two, core, sources, scr, img):
    def fetch(z, nothing):
        for which, source in enumerate(sources):
            if two:
                place = 2 * z + core if which == 0 else 2 * z + 1 - core
            else:
                place = z
            scr[place, :, 0:LANES] = source[z, 0:16, :].astype(jnp.bfloat16)
            scr[place, :, LANES:] = source[z, 16:32, :].astype(jnp.bfloat16)
            img[pl.ds(place, 1), :] = source[z, 32:33, :]
        return nothing

    lax.fori_loop(0, 16, fetch, 0, unroll=4)


def path_kernel(blocks, first, two, numbers_ref, pick, *refs):
    sources, (out_ref, scr, img, ahead, back, costs, ready, starts, states) = refs[:-9], refs[-9:]
    groups = blocks // 4
    lane = lax.broadcasted_iota(jnp.int32, (8, LANES), 1)
    sub = lax.broadcasted_iota(jnp.int32, (8, LANES), 0)
    gather_costs(blocks, two, numbers_ref[8], sources, scr, img)

    place, row = lane[:groups] % 64, sub[:groups]
    line = img[pl.ds(0, groups, stride=4), :]
    for k in range(1, 4):
        line = jnp.where(place // 16 == k, img[pl.ds(k, groups, stride=4), :], line)
    before = pltpu.roll(line, 1, 1)
    wrapped = jnp.concatenate([before[groups - 1 :], before[: groups - 1]], 0)
    before = jnp.where(place == 0, jnp.where(row == 0, 0.0, wrapped), before)
    after = pltpu.roll(line, LANES - 1, 1)
    wrapped = jnp.concatenate([after[1:], after[:1]], 0)
    after = jnp.where(place == 63, jnp.where(row == groups - 1, 0.0, wrapped), after)
    small = [numbers_ref[first + i].astype(jnp.float32) for i in range(2)]
    large = [numbers_ref[4 + first + i].astype(jnp.float32) for i in range(2)]
    ahead[...] = adaptive(small[0], large[0], line - before)
    back[...] = adaptive(small[1], large[1], line - after)
    forward = lane < 64
    penalty_one = jnp.where(forward, small[0], small[1])

    to = lax.broadcasted_iota(jnp.int32, (256, 256), 0)
    of = lax.broadcasted_iota(jnp.int32, (256, 256), 1)
    order = (of == (to % 8) * TILES + to // 8).astype(jnp.bfloat16)
    for g in range(groups):
        pixels = jnp.concatenate(
            [
                scr[4 * g : 4 * g + 4].reshape(64, 256),
                scr[blocks - 4 * g - 4 : blocks - 4 * g].reshape(64, 256),
            ],
            0,
        )
        turned = lax.dot_general(
            order, pixels, (((1,), (1,)), ((), ())), preferred_element_type=jnp.float32
        )
        costs[g] = turned.astype(jnp.bfloat16)

    mirror = jnp.where(lane < 64, 0, LANES - 1)

    def across_sublanes(lowest):
        for shift in (4, 2, 1):
            lowest = jnp.minimum(lowest, pltpu.roll(lowest, shift, 0))
        return lowest

    def halved(level):
        return [jnp.minimum(level[i], level[i + 1]) for i in range(0, len(level), 2)]

    def lowest_of(level):
        while len(level) > 1:
            level = halved(level)
        return across_sublanes(level[0])

    def costs_at(g, i):
        cost = jnp.dot(costs[g], pick[i], preferred_element_type=jnp.float32)
        return cost.reshape(TILES, 8, LANES)

    def penalties(g):
        return jnp.where(
            forward,
            jnp.broadcast_to(ahead[pl.ds(g, 1), :], (8, LANES)),
            jnp.broadcast_to(back[pl.ds(groups - 1 - g, 1), :], (8, LANES)),
        )

    def jump_at(g, i):
        return jnp.take_along_axis(penalties(g), mirror ^ i, axis=1)

    for i in range(AHEAD):
        ready[i] = costs_at(0, i)

    def segments(t, carried):
        *path, jump = carried
        g = t >> 1
        base = (t & 1) << 5
        later = jnp.minimum(t + 1, blocks // 2 - 1)
        lowest = lowest_of(path)
        ordered = penalty_one
        for i in range(32):
            if i % 16 == 0:
                path = [x - lowest for x in path]
                lowest = jnp.zeros_like(lowest)
                here = (lane & 63) == 2 * t + i // 16
                for v in range(TILES):
                    starts[v] = jnp.where(here, path[v], starts[v])
            highest = lowest + (jump if i == 0 else jump_at(g, base + i))
            cost = ready[i] if i < AHEAD else costs_at(g, base + i)
            raised = [x + ordered for x in path]
            below = jnp.where(sub == 0, FAR, pltpu.roll(raised[-1], 1, 0))
            above = jnp.where(sub == 7, FAR, pltpu.roll(raised[0], 7, 0))
            padded = [below, *raised, above]
            near = [
                jnp.minimum(path[v], jnp.minimum(padded[v], padded[v + 2])) for v in range(TILES)
            ]
            path = [jnp.minimum(near[v], highest) + cost[v] for v in range(TILES)]
            pairs = halved(path)
            ordered = jnp.maximum(penalty_one, jnp.minimum(pairs[-1], -FAR))
            lowest = lowest_of(pairs)
            if i == 20:
                jump = jump_at(later >> 1, (later & 1) << 5)
                for k in range(AHEAD):
                    ready[k] = costs_at(later >> 1, ((later & 1) << 5) + k)
        return (*path, jump)

    zero = jnp.zeros((8, LANES), jnp.float32)
    lax.fori_loop(0, blocks // 2, segments, (zero,) * TILES + (jump_at(0, 0),))
    states[...] = jnp.concatenate([starts[:, s, :] for s in range(8)], 0).T
    for z in range(16):
        block = 2 * z + numbers_ref[8] if two else z
        fore, rear = ahead[pl.ds(block // 4, 1), :], back[pl.ds(block // 4, 1), :]
        start, end = states[pl.ds(block, 1), :], states[pl.ds(64 + blocks - 1 - block, 1), :]
        out_ref[z, 0:1, :] = jnp.concatenate([start, fore], 1)
        out_ref[z, 1:2, :] = jnp.concatenate([end, rear], 1)


def path_states(blocks, first, two, numbers, pick, *sources):
    smem = pl.BlockSpec(memory_space=pltpu.SMEM)
    vmem = pl.BlockSpec(memory_space=pltpu.VMEM)
    return pl.pallas_call(
        partial(path_kernel, blocks, first, two),
        out_shape=jax.ShapeDtypeStruct((16, 2, 384), jnp.float32),
        in_specs=[smem] + [vmem] * (1 + len(sources)),
        out_specs=vmem,
        scratch_shapes=[
            pltpu.VMEM((blocks, 16, 256), jnp.bfloat16),
            pltpu.VMEM((blocks, LANES), jnp.float32),
            pltpu.VMEM((blocks // 4, LANES), jnp.float32),
            pltpu.VMEM((blocks // 4, LANES), jnp.float32),
            pltpu.VMEM((blocks // 4, 256, LANES), jnp.bfloat16),
            pltpu.VMEM((AHEAD, TILES, 8, LANES), jnp.float32),
            pltpu.VMEM((TILES, 8, LANES), jnp.float32),
            pltpu.VMEM((LANES, 256), jnp.float32),
        ],
        compiler_params=pltpu.CompilerParams(vmem_limit_bytes=12 * 2**20),
        cost_estimate=pl.CostEstimate(
            flops=blocks * 16 * 256 * 128 * 8, bytes_accessed=blocks * 24 * 1024, transcendentals=0
        ),
        name="line_paths",
    )(numbers, pick, *sources)


def replay_kernel(first, across, numbers_ref, entry_ref, cost_ref, *refs):
    *so_far, out_ref, line, total, jumps = refs
    lane = lax.broadcasted_iota(jnp.int32, (16, 256), 1)
    shift = (LANES - 16 * numbers_ref[9 if across else 10]) % LANES
    cost = cost_ref[...].astype(jnp.float32)
    line[...] = jnp.swapaxes(cost, 0, 1) if across else cost
    total[...] = jnp.zeros_like(total)
    for i in range(2):
        penalty_two = pltpu.roll(entry_ref[:, i, 256:], shift, 1)
        for at in range(16):
            jumps[i, at] = jnp.broadcast_to(penalty_two[:, at : at + 1], (16, LANES))
    small = [numbers_ref[first + i].astype(jnp.float32) for i in range(2)]

    def lowest_of(x):
        return jnp.broadcast_to(jnp.min(x, axis=1, keepdims=True), (16, LANES))

    def wide(x):
        return jnp.concatenate([x, x], 1)

    def step(j, carried):
        after = []
        for i, at in enumerate((j, 15 - j)):
            path, lowest = carried[i]
            cost = line[at]
            below = jnp.where(lane == 0, FAR, pltpu.roll(path, 1, 1))
            above = jnp.where(lane == 255, FAR, pltpu.roll(path, 255, 1))
            near = jnp.minimum(path, jnp.minimum(below, above) + small[i]) + cost
            highest = lowest + jumps[i, at]
            path = jnp.minimum(near, wide(highest) + cost)
            total[at] += path - wide(lowest)
            lowest = jnp.minimum(lowest_of(near), highest + lowest_of(cost))
            after.append((path, lowest))
        return tuple(after)

    paths = [entry_ref[:, i, 0:256] for i in range(2)]
    lax.fori_loop(0, 16, step, tuple((path, lowest_of(path)) for path in paths), unroll=UNROLL)
    if across:
        out_ref[...] = (jnp.swapaxes(total[...], 0, 1) + so_far[0][...]) * OUT_SCALE
    else:
        out_ref[...] = total[...]


def replay(first, across, numbers, entry, cost, *so_far):
    smem = pl.BlockSpec(memory_space=pltpu.SMEM)
    vmem = pl.BlockSpec(memory_space=pltpu.VMEM)
    return pl.pallas_call(
        partial(replay_kernel, first, across),
        out_shape=jax.ShapeDtypeStruct((16, 16, 256), jnp.float32),
        in_specs=[smem] + [vmem] * (2 + len(so_far)),
        out_specs=vmem,
        scratch_shapes=[
            pltpu.VMEM((16, 16, 256), jnp.float32),
            pltpu.VMEM((16, 16, 256), jnp.float32),
            pltpu.VMEM((2, 16, 16, LANES), jnp.float32),
        ],
        cost_estimate=pl.CostEstimate(
            flops=2 * 65536 * 100, bytes_accessed=2**20, transcendentals=0
        ),
        compiler_params=pltpu.CompilerParams(vmem_limit_bytes=3 * 2**20),
        name="block_paths",
    )(numbers, entry, cost, *so_far)


def message(cost, image):
    wide = jnp.tile(image, (1, LANES // 16))[:, None, :]
    empty = jnp.zeros((16, ROWS - 33, LANES), jnp.float32)
    cost = cost.astype(jnp.float32)
    return jnp.concatenate([cost[:, :, :LANES], cost[:, :, LANES:], wide, empty], 1)


def after_kernel(value_ref, earlier_ref, out_ref):
    out_ref[...] = value_ref[...]


def after(value, earlier):
    vmem = pl.BlockSpec(memory_space=pltpu.VMEM)
    return pl.pallas_call(
        after_kernel,
        out_shape=jax.ShapeDtypeStruct(value.shape, value.dtype),
        in_specs=[vmem] * 2,
        out_specs=vmem,
        compiler_params=pltpu.CompilerParams(vmem_limit_bytes=2 * 2**20),
        name="after",
    )(value, earlier)


def on_device(cost_volume, left_image, p_small, p_large):
    index_x, index_y = lax.axis_index("gx"), lax.axis_index("gy")
    here = jnp.stack([index_x % 2, index_x % 4, index_y % 4]).astype(jnp.int32)
    numbers = jnp.concatenate([p_small, p_large, here])
    step, pixel, path = (lax.broadcasted_iota(jnp.int32, (64, LANES, LANES), i) for i in range(3))
    pick = (pixel == jnp.where(path < 64, step, LANES - 1 - step)).astype(jnp.bfloat16)
    chips = [[2 * z + c for z in range(16)] for c in range(2)]
    swap = [(i, i ^ 1) for i in range(32)]

    columns = message(jnp.transpose(cost_volume, (1, 0, 2)), left_image.T)
    lines = message(cost_volume, left_image)
    columns = lax.all_to_all(columns, "gy", 0, 0)
    lines = after(lines, columns)
    lines = lax.all_to_all(lines, "gx", 0, 0, axis_index_groups=chips)
    entry_y = path_states(16, 2, False, numbers, pick, columns)
    lines = after(lines, entry_y)
    others = lax.ppermute(lines, "gx", swap)

    entry_y = lax.all_to_all(entry_y, "gy", 0, 0)
    entry_x = path_states(32, 0, True, numbers, pick, lines, others)
    entry_x = lax.all_to_all(entry_x, "gx", 0, 0, axis_index_groups=chips)

    total = replay(2, False, numbers, entry_y, cost_volume)
    return replay(0, True, numbers, entry_x, cost_volume, total)


def solution(mesh):
    in_specs = (P("gy", "gx", None), P("gy", "gx"), P(), P())
    out_specs = P("gy", "gx", None)
    return jax.shard_map(
        on_device, mesh=mesh, in_specs=in_specs, out_specs=out_specs, check_vma=False
    )
```

```python
from functools import partial

import jax
import jax.numpy as jnp
from jax import lax
from jax.experimental import pallas as pl
from jax.experimental.pallas import tpu as pltpu
from jax.sharding import PartitionSpec as P

FAR = 1e30
GRADIENT_GAIN = 4.0
OUT_SCALE = 1.0 / 256.0
LANES = 128
TILES = 32
UNROLL = 4
AHEAD = 3
ROWS = 40


def adaptive(penalty_one, penalty_two, step_diff):
    return penalty_one + (penalty_two - penalty_one) / (1.0 + GRADIENT_GAIN * jnp.abs(step_diff))


def gather_costs(blocks, two, core, sources, scr, img):
    def fetch(z, nothing):
        for which, source in enumerate(sources):
            if two:
                place = 2 * z + core if which == 0 else 2 * z + 1 - core
            else:
                place = z
            scr[place, :, 0:LANES] = source[z, 0:16, :].astype(jnp.bfloat16)
            scr[place, :, LANES:] = source[z, 16:32, :].astype(jnp.bfloat16)
            img[pl.ds(place, 1), :] = source[z, 32:33, :]
        return nothing

    lax.fori_loop(0, 16, fetch, 0, unroll=4)


def path_kernel(blocks, first, two, numbers_ref, pick, *refs):
    sources, (out_ref, scr, img, ahead, back, costs, ready, starts, states) = refs[:-9], refs[-9:]
    groups = blocks // 4
    lane = lax.broadcasted_iota(jnp.int32, (8, LANES), 1)
    sub = lax.broadcasted_iota(jnp.int32, (8, LANES), 0)
    gather_costs(blocks, two, numbers_ref[8], sources, scr, img)

    place, row = lane[:groups] % 64, sub[:groups]
    line = img[pl.ds(0, groups, stride=4), :]
    for k in range(1, 4):
        line = jnp.where(place // 16 == k, img[pl.ds(k, groups, stride=4), :], line)
    before = pltpu.roll(line, 1, 1)
    wrapped = jnp.concatenate([before[groups - 1 :], before[: groups - 1]], 0)
    before = jnp.where(place == 0, jnp.where(row == 0, 0.0, wrapped), before)
    after = pltpu.roll(line, LANES - 1, 1)
    wrapped = jnp.concatenate([after[1:], after[:1]], 0)
    after = jnp.where(place == 63, jnp.where(row == groups - 1, 0.0, wrapped), after)
    small = [numbers_ref[first + i].astype(jnp.float32) for i in range(2)]
    large = [numbers_ref[4 + first + i].astype(jnp.float32) for i in range(2)]
    ahead[...] = adaptive(small[0], large[0], line - before)
    back[...] = adaptive(small[1], large[1], line - after)
    forward = lane < 64
    penalty_one = jnp.where(forward, small[0], small[1])

    to = lax.broadcasted_iota(jnp.int32, (256, 256), 0)
    of = lax.broadcasted_iota(jnp.int32, (256, 256), 1)
    order = (of == (to % 8) * TILES + to // 8).astype(jnp.bfloat16)
    for g in range(groups):
        pixels = jnp.concatenate(
            [
                scr[4 * g : 4 * g + 4].reshape(64, 256),
                scr[blocks - 4 * g - 4 : blocks - 4 * g].reshape(64, 256),
            ],
            0,
        )
        turned = lax.dot_general(
            order, pixels, (((1,), (1,)), ((), ())), preferred_element_type=jnp.float32
        )
        costs[g] = turned.astype(jnp.bfloat16)

    mirror = jnp.where(lane < 64, 0, LANES - 1)

    def across_sublanes(lowest):
        for shift in (4, 2, 1):
            lowest = jnp.minimum(lowest, pltpu.roll(lowest, shift, 0))
        return lowest

    def halved(level):
        return [jnp.minimum(level[i], level[i + 1]) for i in range(0, len(level), 2)]

    def lowest_of(level):
        while len(level) > 1:
            level = halved(level)
        return across_sublanes(level[0])

    def costs_at(g, i):
        cost = jnp.dot(costs[g], pick[i], preferred_element_type=jnp.float32)
        return cost.reshape(TILES, 8, LANES)

    def penalties(g):
        return jnp.where(
            forward,
            jnp.broadcast_to(ahead[pl.ds(g, 1), :], (8, LANES)),
            jnp.broadcast_to(back[pl.ds(groups - 1 - g, 1), :], (8, LANES)),
        )

    def jump_at(g, i):
        return jnp.take_along_axis(penalties(g), mirror ^ i, axis=1)

    for i in range(AHEAD):
        ready[i] = costs_at(0, i)

    def segments(t, carried):
        *path, jump = carried
        g = t >> 1
        base = (t & 1) << 5
        later = jnp.minimum(t + 1, blocks // 2 - 1)
        lowest = lowest_of(path)
        ordered = penalty_one
        for i in range(32):
            if i % 16 == 0:
                path = [x - lowest for x in path]
                lowest = jnp.zeros_like(lowest)
                here = (lane & 63) == 2 * t + i // 16
                for v in range(TILES):
                    starts[v] = jnp.where(here, path[v], starts[v])
            highest = lowest + (jump if i == 0 else jump_at(g, base + i))
            cost = ready[i] if i < AHEAD else costs_at(g, base + i)
            raised = [x + ordered for x in path]
            below = jnp.where(sub == 0, FAR, pltpu.roll(raised[-1], 1, 0))
            above = jnp.where(sub == 7, FAR, pltpu.roll(raised[0], 7, 0))
            padded = [below, *raised, above]
            near = [
                jnp.minimum(path[v], jnp.minimum(padded[v], padded[v + 2])) for v in range(TILES)
            ]
            path = [jnp.minimum(near[v], highest) + cost[v] for v in range(TILES)]
            pairs = halved(path)
            ordered = jnp.maximum(penalty_one, jnp.minimum(pairs[-1], -FAR))
            lowest = lowest_of(pairs)
            if i == 20:
                jump = jump_at(later >> 1, (later & 1) << 5)
                for k in range(AHEAD):
                    ready[k] = costs_at(later >> 1, ((later & 1) << 5) + k)
        return (*path, jump)

    zero = jnp.zeros((8, LANES), jnp.float32)
    lax.fori_loop(0, blocks // 2, segments, (zero,) * TILES + (jump_at(0, 0),))
    states[...] = jnp.concatenate([starts[:, s, :] for s in range(8)], 0).T
    for z in range(16):
        block = 2 * z + numbers_ref[8] if two else z
        fore, rear = ahead[pl.ds(block // 4, 1), :], back[pl.ds(block // 4, 1), :]
        start, end = states[pl.ds(block, 1), :], states[pl.ds(64 + blocks - 1 - block, 1), :]
        out_ref[z, 0:1, :] = jnp.concatenate([start, fore], 1)
        out_ref[z, 1:2, :] = jnp.concatenate([end, rear], 1)


def path_states(blocks, first, two, numbers, pick, *sources):
    smem = pl.BlockSpec(memory_space=pltpu.SMEM)
    vmem = pl.BlockSpec(memory_space=pltpu.VMEM)
    return pl.pallas_call(
        partial(path_kernel, blocks, first, two),
        out_shape=jax.ShapeDtypeStruct((16, 2, 384), jnp.float32),
        in_specs=[smem] + [vmem] * (1 + len(sources)),
        out_specs=vmem,
        scratch_shapes=[
            pltpu.VMEM((blocks, 16, 256), jnp.bfloat16),
            pltpu.VMEM((blocks, LANES), jnp.float32),
            pltpu.VMEM((blocks // 4, LANES), jnp.float32),
            pltpu.VMEM((blocks // 4, LANES), jnp.float32),
            pltpu.VMEM((blocks // 4, 256, LANES), jnp.bfloat16),
            pltpu.VMEM((AHEAD, TILES, 8, LANES), jnp.float32),
            pltpu.VMEM((TILES, 8, LANES), jnp.float32),
            pltpu.VMEM((LANES, 256), jnp.float32),
        ],
        compiler_params=pltpu.CompilerParams(vmem_limit_bytes=12 * 2**20),
        cost_estimate=pl.CostEstimate(
            flops=blocks * 16 * 256 * 128 * 8, bytes_accessed=blocks * 24 * 1024, transcendentals=0
        ),
        name="line_paths",
    )(numbers, pick, *sources)


def replay_kernel(first, across, numbers_ref, entry_ref, cost_ref, *refs):
    *so_far, out_ref, line, total, jumps = refs
    lane = lax.broadcasted_iota(jnp.int32, (16, 256), 1)
    shift = (LANES - 16 * numbers_ref[9 if across else 10]) % LANES
    cost = cost_ref[...].astype(jnp.float32)
    line[...] = jnp.swapaxes(cost, 0, 1) if across else cost
    total[...] = jnp.zeros_like(total)
    for i in range(2):
        penalty_two = pltpu.roll(entry_ref[:, i, 256:], shift, 1)
        for at in range(16):
            jumps[i, at] = jnp.broadcast_to(penalty_two[:, at : at + 1], (16, LANES))
    small = [numbers_ref[first + i].astype(jnp.float32) for i in range(2)]

    def lowest_of(x):
        return jnp.broadcast_to(jnp.min(x, axis=1, keepdims=True), (16, LANES))

    def wide(x):
        return jnp.concatenate([x, x], 1)

    def step(j, carried):
        after = []
        for i, at in enumerate((j, 15 - j)):
            path, lowest = carried[i]
            cost = line[at]
            below = jnp.where(lane == 0, FAR, pltpu.roll(path, 1, 1))
            above = jnp.where(lane == 255, FAR, pltpu.roll(path, 255, 1))
            near = jnp.minimum(path, jnp.minimum(below, above) + small[i]) + cost
            highest = lowest + jumps[i, at]
            path = jnp.minimum(near, wide(highest) + cost)
            total[at] += path - wide(lowest)
            lowest = jnp.minimum(lowest_of(near), highest + lowest_of(cost))
            after.append((path, lowest))
        return tuple(after)

    paths = [entry_ref[:, i, 0:256] for i in range(2)]
    lax.fori_loop(0, 16, step, tuple((path, lowest_of(path)) for path in paths), unroll=UNROLL)
    if across:
        out_ref[...] = (jnp.swapaxes(total[...], 0, 1) + so_far[0][...]) * OUT_SCALE
    else:
        out_ref[...] = total[...]


def replay(first, across, numbers, entry, cost, *so_far):
    smem = pl.BlockSpec(memory_space=pltpu.SMEM)
    vmem = pl.BlockSpec(memory_space=pltpu.VMEM)
    return pl.pallas_call(
        partial(replay_kernel, first, across),
        out_shape=jax.ShapeDtypeStruct((16, 16, 256), jnp.float32),
        in_specs=[smem] + [vmem] * (2 + len(so_far)),
        out_specs=vmem,
        scratch_shapes=[
            pltpu.VMEM((16, 16, 256), jnp.float32),
            pltpu.VMEM((16, 16, 256), jnp.float32),
            pltpu.VMEM((2, 16, 16, LANES), jnp.float32),
        ],
        cost_estimate=pl.CostEstimate(
            flops=2 * 65536 * 100, bytes_accessed=2**20, transcendentals=0
        ),
        compiler_params=pltpu.CompilerParams(vmem_limit_bytes=3 * 2**20),
        name="block_paths",
    )(numbers, entry, cost, *so_far)


def column_message_kernel(cost_ref, image_ref, out_ref):
    crossed = jnp.swapaxes(cost_ref[...].astype(jnp.float32), 0, 1)
    out_ref[:, 0:16, :] = crossed[:, :, 0:LANES]
    out_ref[:, 16:32, :] = crossed[:, :, LANES:]
    row = lax.broadcasted_iota(jnp.int32, (16, LANES), 0)
    lane = lax.broadcasted_iota(jnp.int32, (16, LANES), 1)
    image = image_ref[...]
    for c in range(16):
        column = jnp.where(lane % 16 == row, image[:, c : c + 1], 0.0)
        line = jnp.sum(column, axis=0, keepdims=True)
        out_ref[c, 32:40, :] = jnp.broadcast_to(line, (8, LANES))


def column_message(cost, image):
    vmem = pl.BlockSpec(memory_space=pltpu.VMEM)
    return pl.pallas_call(
        column_message_kernel,
        out_shape=jax.ShapeDtypeStruct((16, ROWS, LANES), jnp.float32),
        in_specs=[vmem] * 2,
        out_specs=vmem,
        compiler_params=pltpu.CompilerParams(vmem_limit_bytes=3 * 2**20),
        name="column_message",
    )(cost, image)


def message(cost, image):
    wide = jnp.tile(image, (1, LANES // 16))[:, None, :]
    empty = jnp.zeros((16, ROWS - 33, LANES), jnp.float32)
    cost = cost.astype(jnp.float32)
    return jnp.concatenate([cost[:, :, :LANES], cost[:, :, LANES:], wide, empty], 1)


def after_kernel(value_ref, earlier_ref, out_ref):
    out_ref[...] = value_ref[...]


def after(value, earlier, space):
    vmem = pl.BlockSpec(memory_space=pltpu.VMEM)
    return pl.pallas_call(
        after_kernel,
        out_shape=jax.ShapeDtypeStruct(value.shape, value.dtype),
        in_specs=[vmem, pl.BlockSpec(memory_space=space)],
        out_specs=vmem,
        compiler_params=pltpu.CompilerParams(vmem_limit_bytes=2 * 2**20),
        name="after",
    )(value, earlier)


def on_device(cost_volume, left_image, p_small, p_large):
    index_x, index_y = lax.axis_index("gx"), lax.axis_index("gy")
    here = jnp.stack([index_x % 2, index_x % 4, index_y % 4]).astype(jnp.int32)
    numbers = jnp.concatenate([p_small, p_large, here])
    step, pixel, path = (lax.broadcasted_iota(jnp.int32, (64, LANES, LANES), i) for i in range(3))
    pick = (pixel == jnp.where(path < 64, step, LANES - 1 - step)).astype(jnp.bfloat16)
    chips = [[2 * z + c for z in range(16)] for c in range(2)]
    swap = [(i, i ^ 1) for i in range(32)]

    columns = column_message(cost_volume, left_image)
    lines = message(cost_volume, left_image)
    columns = lax.all_to_all(columns, "gy", 0, 0)
    lines = after(lines, columns, pltpu.VMEM)
    lines = lax.all_to_all(lines, "gx", 0, 0, axis_index_groups=chips)
    entry_y = path_states(16, 2, False, numbers, pick, columns)
    lines = after(lines, entry_y, pl.ANY)
    others = lax.ppermute(lines, "gx", swap)

    entry_y = lax.all_to_all(entry_y, "gy", 0, 0)
    entry_x = path_states(32, 0, True, numbers, pick, lines, others)
    entry_x = lax.all_to_all(entry_x, "gx", 0, 0, axis_index_groups=chips)

    total = replay(2, False, numbers, entry_y, cost_volume)
    return replay(0, True, numbers, entry_x, cost_volume, total)


def solution(mesh):
    in_specs = (P("gy", "gx", None), P("gy", "gx"), P(), P())
    out_specs = P("gy", "gx", None)
    return jax.shard_map(
        on_device, mesh=mesh, in_specs=in_specs, out_specs=out_specs, check_vma=False
    )
```

```python
from functools import partial

import jax
import jax.numpy as jnp
from jax import lax
from jax.experimental import pallas as pl
from jax.experimental.pallas import tpu as pltpu
from jax.sharding import PartitionSpec as P

FAR = 1e30
GRADIENT_GAIN = 4.0
OUT_SCALE = 1.0 / 256.0
LANES = 128
TILES = 32
UNROLL = 4
AHEAD = 3
ROWS = 40


def adaptive(penalty_one, penalty_two, step_diff):
    return penalty_one + (penalty_two - penalty_one) / (1.0 + GRADIENT_GAIN * jnp.abs(step_diff))


def taken(values, lanes):
    return jnp.take_along_axis(values, lanes, axis=1, mode="promise_in_bounds")


def gather_costs(blocks, two, core, sources, scr, img):
    def fetch(z, nothing):
        for which, source in enumerate(sources):
            if two:
                place = 2 * z + core if which == 0 else 2 * z + 1 - core
            else:
                place = z
            scr[place, :, 0:LANES] = source[z, 0:16, :].astype(jnp.bfloat16)
            scr[place, :, LANES:] = source[z, 16:32, :].astype(jnp.bfloat16)
            img[pl.ds(place, 1), :] = source[z, 32:33, :]
        return nothing

    lax.fori_loop(0, 16, fetch, 0, unroll=4)


def path_kernel(blocks, first, two, numbers_ref, pick, *refs):
    sources, (out_ref, scr, img, ahead, back, costs, ready, starts, states) = refs[:-9], refs[-9:]
    groups = blocks // 4
    lane = lax.broadcasted_iota(jnp.int32, (8, LANES), 1)
    sub = lax.broadcasted_iota(jnp.int32, (8, LANES), 0)
    gather_costs(blocks, two, numbers_ref[8], sources, scr, img)

    place, row = lane[:groups] % 64, sub[:groups]
    line = img[pl.ds(0, groups, stride=4), :]
    for k in range(1, 4):
        line = jnp.where(place // 16 == k, img[pl.ds(k, groups, stride=4), :], line)
    before = pltpu.roll(line, 1, 1)
    wrapped = jnp.concatenate([before[groups - 1 :], before[: groups - 1]], 0)
    before = jnp.where(place == 0, jnp.where(row == 0, 0.0, wrapped), before)
    after = pltpu.roll(line, LANES - 1, 1)
    wrapped = jnp.concatenate([after[1:], after[:1]], 0)
    after = jnp.where(place == 63, jnp.where(row == groups - 1, 0.0, wrapped), after)
    small = [numbers_ref[first + i].astype(jnp.float32) for i in range(2)]
    large = [numbers_ref[4 + first + i].astype(jnp.float32) for i in range(2)]
    ahead[...] = adaptive(small[0], large[0], line - before)
    back[...] = adaptive(small[1], large[1], line - after)
    forward = lane < 64
    penalty_one = jnp.where(forward, small[0], small[1])

    to = lax.broadcasted_iota(jnp.int32, (256, 256), 0)
    of = lax.broadcasted_iota(jnp.int32, (256, 256), 1)
    order = (of == (to % 8) * TILES + to // 8).astype(jnp.bfloat16)
    for g in range(groups):
        pixels = jnp.concatenate(
            [
                scr[4 * g : 4 * g + 4].reshape(64, 256),
                scr[blocks - 4 * g - 4 : blocks - 4 * g].reshape(64, 256),
            ],
            0,
        )
        turned = lax.dot_general(
            order, pixels, (((1,), (1,)), ((), ())), preferred_element_type=jnp.float32
        )
        costs[g] = turned.astype(jnp.bfloat16)

    mirror = jnp.where(lane < 64, 0, LANES - 1)

    def across_sublanes(lowest):
        for shift in (4, 2, 1):
            lowest = jnp.minimum(lowest, pltpu.roll(lowest, shift, 0))
        return lowest

    def halved(level):
        return [jnp.minimum(level[i], level[i + 1]) for i in range(0, len(level), 2)]

    def lowest_of(level):
        while len(level) > 1:
            level = halved(level)
        return across_sublanes(level[0])

    def costs_at(g, i):
        cost = jnp.dot(costs[g], pick[i], preferred_element_type=jnp.float32)
        return cost.reshape(TILES, 8, LANES)

    def penalties(g):
        return jnp.where(
            forward,
            jnp.broadcast_to(ahead[pl.ds(g, 1), :], (8, LANES)),
            jnp.broadcast_to(back[pl.ds(groups - 1 - g, 1), :], (8, LANES)),
        )

    def jump_at(g, i):
        return taken(penalties(g), mirror ^ i)

    for i in range(AHEAD):
        ready[i] = costs_at(0, i)

    def segments(t, carried):
        *path, jump = carried
        g = t >> 1
        base = (t & 1) << 5
        later = jnp.minimum(t + 1, blocks // 2 - 1)
        lowest = lowest_of(path)
        ordered = penalty_one
        for i in range(32):
            if i % 16 == 0:
                path = [x - lowest for x in path]
                lowest = jnp.zeros_like(lowest)
                here = (lane & 63) == 2 * t + i // 16
                for v in range(TILES):
                    starts[v] = jnp.where(here, path[v], starts[v])
            highest = lowest + (jump if i == 0 else jump_at(g, base + i))
            cost = ready[i] if i < AHEAD else costs_at(g, base + i)
            raised = [x + ordered for x in path]
            below = jnp.where(sub == 0, FAR, pltpu.roll(raised[-1], 1, 0))
            above = jnp.where(sub == 7, FAR, pltpu.roll(raised[0], 7, 0))
            padded = [below, *raised, above]
            near = [
                jnp.minimum(path[v], jnp.minimum(padded[v], padded[v + 2])) for v in range(TILES)
            ]
            path = [jnp.minimum(near[v], highest) + cost[v] for v in range(TILES)]
            pairs = halved(path)
            ordered = jnp.maximum(penalty_one, jnp.minimum(pairs[-1], -FAR))
            lowest = lowest_of(pairs)
            if i == 20:
                jump = jump_at(later >> 1, (later & 1) << 5)
                for k in range(AHEAD):
                    ready[k] = costs_at(later >> 1, ((later & 1) << 5) + k)
        return (*path, jump)

    zero = jnp.zeros((8, LANES), jnp.float32)
    lax.fori_loop(0, blocks // 2, segments, (zero,) * TILES + (jump_at(0, 0),))
    states[...] = jnp.concatenate([starts[:, s, :] for s in range(8)], 0).T
    for z in range(16):
        block = 2 * z + numbers_ref[8] if two else z
        fore, rear = ahead[pl.ds(block // 4, 1), :], back[pl.ds(block // 4, 1), :]
        start, end = states[pl.ds(block, 1), :], states[pl.ds(64 + blocks - 1 - block, 1), :]
        out_ref[z, 0:1, :] = jnp.concatenate([start, fore], 1)
        out_ref[z, 1:2, :] = jnp.concatenate([end, rear], 1)


def path_states(blocks, first, two, numbers, pick, *sources):
    smem = pl.BlockSpec(memory_space=pltpu.SMEM)
    vmem = pl.BlockSpec(memory_space=pltpu.VMEM)
    return pl.pallas_call(
        partial(path_kernel, blocks, first, two),
        out_shape=jax.ShapeDtypeStruct((16, 2, 384), jnp.float32),
        in_specs=[smem] + [vmem] * (1 + len(sources)),
        out_specs=vmem,
        scratch_shapes=[
            pltpu.VMEM((blocks, 16, 256), jnp.bfloat16),
            pltpu.VMEM((blocks, LANES), jnp.float32),
            pltpu.VMEM((blocks // 4, LANES), jnp.float32),
            pltpu.VMEM((blocks // 4, LANES), jnp.float32),
            pltpu.VMEM((blocks // 4, 256, LANES), jnp.bfloat16),
            pltpu.VMEM((AHEAD, TILES, 8, LANES), jnp.float32),
            pltpu.VMEM((TILES, 8, LANES), jnp.float32),
            pltpu.VMEM((LANES, 256), jnp.float32),
        ],
        compiler_params=pltpu.CompilerParams(vmem_limit_bytes=12 * 2**20),
        cost_estimate=pl.CostEstimate(
            flops=blocks * 16 * 256 * 128 * 8, bytes_accessed=blocks * 24 * 1024, transcendentals=0
        ),
        name="line_paths",
    )(numbers, pick, *sources)


def replay_steps(first, place, rows_ref, entry_ref, line, total, jumps):
    lane = lax.broadcasted_iota(jnp.int32, (16, 256), 1)
    offset = 16 * rows_ref[place : place + 1, :]
    for i in range(2):
        for at in range(16):
            source = jnp.broadcast_to(offset + at, (16, LANES))
            jumps[i, at] = taken(entry_ref[:, i, 256:], source)

    def lowest_of(x):
        return jnp.broadcast_to(jnp.min(x, axis=1, keepdims=True), (16, LANES))

    def wide(x):
        return jnp.concatenate([x, x], 1)

    small = [wide(rows_ref[first + i : first + i + 1, :].astype(jnp.float32)) for i in range(2)]

    def step(j, carried):
        done = []
        for i, at in enumerate((j, 15 - j)):
            path, lowest = carried[i]
            cost = line[at]
            below = jnp.where(lane == 0, FAR, pltpu.roll(path, 1, 1))
            above = jnp.where(lane == 255, FAR, pltpu.roll(path, 255, 1))
            near = jnp.minimum(path, jnp.minimum(below, above) + small[i]) + cost
            highest = lowest + jumps[i, at]
            path = jnp.minimum(near, wide(highest) + cost)
            total[at] += path - wide(lowest)
            lowest = jnp.minimum(lowest_of(near), highest + lowest_of(cost))
            done.append((path, lowest))
        return tuple(done)

    paths = [entry_ref[:, i, 0:256] for i in range(2)]
    lax.fori_loop(0, 16, step, tuple((path, lowest_of(path)) for path in paths), unroll=UNROLL)


def columns_replay_kernel(rows_ref, entry_ref, cost_ref, sum_ref, line_ref, line, total, jumps):
    cost = cost_ref[...].astype(jnp.float32)
    line[...] = cost
    total[...] = jnp.zeros_like(total)
    replay_steps(2, 10, rows_ref, entry_ref, line, total, jumps)
    sum_ref[...] = jnp.swapaxes(total[...], 0, 1)
    line_ref[...] = jnp.swapaxes(cost, 0, 1)


def lines_replay_kernel(rows_ref, entry_ref, sum_ref, line_ref, out_ref, total, jumps):
    total[...] = sum_ref[...]
    replay_steps(0, 9, rows_ref, entry_ref, line_ref, total, jumps)
    out_ref[...] = jnp.swapaxes(total[...], 0, 1) * OUT_SCALE


def replay(kernel, outs, *operands):
    block = jax.ShapeDtypeStruct((16, 16, 256), jnp.float32)
    vmem = pl.BlockSpec(memory_space=pltpu.VMEM)
    return pl.pallas_call(
        kernel,
        out_shape=[block] * outs,
        in_specs=[vmem] * len(operands),
        out_specs=[vmem] * outs,
        scratch_shapes=[pltpu.VMEM(block.shape, block.dtype)] * outs
        + [pltpu.VMEM((2, 16, 16, LANES), jnp.float32)],
        cost_estimate=pl.CostEstimate(
            flops=2 * 65536 * 100, bytes_accessed=2**20, transcendentals=0
        ),
        compiler_params=pltpu.CompilerParams(vmem_limit_bytes=4 * 2**20),
        name="block_paths",
    )(*operands)


def column_message_kernel(cost_hbm, image_hbm, out_ref, cost_ref, image_ref, cost_sem, image_sem):
    cost_copy = pltpu.make_async_copy(cost_hbm, cost_ref, cost_sem)
    image_copy = pltpu.make_async_copy(image_hbm, image_ref, image_sem)
    cost_copy.start()
    image_copy.start()
    cost_copy.wait()
    image_copy.wait()
    crossed = jnp.swapaxes(cost_ref[...].astype(jnp.float32), 0, 1)
    out_ref[:, 0:16, :] = crossed[:, :, 0:LANES]
    out_ref[:, 16:32, :] = crossed[:, :, LANES:]
    row = lax.broadcasted_iota(jnp.int32, (16, LANES), 0)
    lane = lax.broadcasted_iota(jnp.int32, (16, LANES), 1)
    image = image_ref[...]
    for c in range(16):
        column = jnp.where(lane % 16 == row, image[:, c : c + 1], 0.0)
        line = jnp.sum(column, axis=0, keepdims=True)
        out_ref[c, 32:40, :] = jnp.broadcast_to(line, (8, LANES))


def column_message(cost, image):
    return pl.pallas_call(
        column_message_kernel,
        out_shape=jax.ShapeDtypeStruct((16, ROWS, LANES), jnp.float32),
        in_specs=[pl.BlockSpec(memory_space=pltpu.HBM)] * 2,
        out_specs=pl.BlockSpec(memory_space=pltpu.VMEM),
        scratch_shapes=[
            pltpu.VMEM((16, 16, 256), jnp.int32),
            pltpu.VMEM((16, 16), jnp.float32),
            pltpu.SemaphoreType.DMA,
            pltpu.SemaphoreType.DMA,
        ],
        compiler_params=pltpu.CompilerParams(vmem_limit_bytes=56 * 2**20),
        name="column_message",
    )(cost, image)


def message(cost, image):
    wide = jnp.tile(image, (1, LANES // 16))[:, None, :]
    empty = jnp.zeros((16, ROWS - 33, LANES), jnp.float32)
    cost = cost.astype(jnp.float32)
    return jnp.concatenate([cost[:, :, :LANES], cost[:, :, LANES:], wide, empty], 1)


def after_kernel(value_ref, earlier_ref, out_ref):
    out_ref[...] = value_ref[...]


def pass_kernel(value_ref, earlier_ref, out_ref):
    pass


def passed_after(value, earlier):
    return pl.pallas_call(
        pass_kernel,
        out_shape=jax.ShapeDtypeStruct(value.shape, value.dtype),
        in_specs=[pl.BlockSpec(memory_space=pl.ANY), pl.BlockSpec(memory_space=pltpu.VMEM)],
        out_specs=pl.BlockSpec(memory_space=pl.ANY),
        input_output_aliases={0: 0},
        compiler_params=pltpu.CompilerParams(vmem_limit_bytes=2 * 2**20),
        name="passed_after",
    )(value, earlier)


def after(value, earlier):
    vmem = pl.BlockSpec(memory_space=pltpu.VMEM)
    return pl.pallas_call(
        after_kernel,
        out_shape=jax.ShapeDtypeStruct(value.shape, value.dtype),
        in_specs=[vmem, pl.BlockSpec(memory_space=pl.ANY)],
        out_specs=vmem,
        compiler_params=pltpu.CompilerParams(vmem_limit_bytes=2 * 2**20),
        name="after",
    )(value, earlier)


def on_device(cost_volume, left_image, p_small, p_large):
    index_x, index_y = lax.axis_index("gx"), lax.axis_index("gy")
    here = jnp.stack([index_x % 2, index_x % 4, index_y % 4]).astype(jnp.int32)
    numbers = jnp.concatenate([p_small, p_large, here])
    rows = jnp.broadcast_to(jnp.pad(numbers, (0, 5))[:, None], (16, LANES))
    step, pixel, path = (lax.broadcasted_iota(jnp.int32, (64, LANES, LANES), i) for i in range(3))
    pick = (pixel == jnp.where(path < 64, step, LANES - 1 - step)).astype(jnp.bfloat16)
    chips = [[2 * z + c for z in range(16)] for c in range(2)]
    swap = [(i, i ^ 1) for i in range(32)]

    columns = column_message(cost_volume, left_image)
    lines = message(cost_volume, left_image)
    columns = lax.all_to_all(columns, "gy", 0, 0)
    lines = passed_after(lines, columns)
    lines = lax.all_to_all(lines, "gx", 0, 0, axis_index_groups=chips)
    entry_y = path_states(16, 2, False, numbers, pick, columns)
    lines = after(lines, entry_y)
    others = lax.ppermute(lines, "gx", swap)

    entry_y = lax.all_to_all(entry_y, "gy", 0, 0)
    entry_x = path_states(32, 0, True, numbers, pick, lines, others)
    entry_x = lax.all_to_all(entry_x, "gx", 0, 0, axis_index_groups=chips)

    total, line = replay(columns_replay_kernel, 2, rows, entry_y, cost_volume)
    return replay(lines_replay_kernel, 1, rows, entry_x, total, line)[0]


def solution(mesh):
    in_specs = (P("gy", "gx", None), P("gy", "gx"), P(), P())
    out_specs = P("gy", "gx", None)
    return jax.shard_map(
        on_device, mesh=mesh, in_specs=in_specs, out_specs=out_specs, check_vma=False
    )
```

```python
from functools import partial

import jax
import jax.numpy as jnp
from jax import lax
from jax.experimental import pallas as pl
from jax.experimental.pallas import tpu as pltpu
from jax.sharding import PartitionSpec as P

FAR = 1e30
GRADIENT_GAIN = 4.0
OUT_SCALE = 1.0 / 256.0
LANES = 128
TILES = 32
UNROLL = 4
AHEAD = 4
ROWS = 40


def adaptive(penalty_one, penalty_two, step_diff):
    return penalty_one + (penalty_two - penalty_one) / (1.0 + GRADIENT_GAIN * jnp.abs(step_diff))


def taken(values, lanes):
    return jnp.take_along_axis(values, lanes, axis=1, mode="promise_in_bounds")


def gather_costs(blocks, two, core, sources, scr, img):
    def fetch(z, nothing):
        for which, source in enumerate(sources):
            if two:
                place = 2 * z + core if which == 0 else 2 * z + 1 - core
            else:
                place = z
            scr[place, :, 0:LANES] = source[z, 0:16, :].astype(jnp.bfloat16)
            scr[place, :, LANES:] = source[z, 16:32, :].astype(jnp.bfloat16)
            img[pl.ds(place, 1), :] = source[z, 32:33, :]
        return nothing

    lax.fori_loop(0, 16, fetch, 0, unroll=4)


def path_kernel(blocks, first, two, rows_ref, pick, *refs):
    sources, (out_ref, scr, img, ahead, back, costs, ready, starts, states) = refs[:-9], refs[-9:]
    groups = blocks // 4
    lane = lax.broadcasted_iota(jnp.int32, (8, LANES), 1)
    sub = lax.broadcasted_iota(jnp.int32, (8, LANES), 0)
    core = lax.axis_index("gx") % 2 if two else 0
    gather_costs(blocks, two, core, sources, scr, img)

    place, row = lane[:groups] % 64, sub[:groups]
    line = img[pl.ds(0, groups, stride=4), :]
    for k in range(1, 4):
        line = jnp.where(place // 16 == k, img[pl.ds(k, groups, stride=4), :], line)
    before = pltpu.roll(line, 1, 1)
    wrapped = jnp.concatenate([before[groups - 1 :], before[: groups - 1]], 0)
    before = jnp.where(place == 0, jnp.where(row == 0, 0.0, wrapped), before)
    after = pltpu.roll(line, LANES - 1, 1)
    wrapped = jnp.concatenate([after[1:], after[:1]], 0)
    after = jnp.where(place == 63, jnp.where(row == groups - 1, 0.0, wrapped), after)
    small, large = (
        [rows_ref[at + i : at + i + 1, :].astype(jnp.float32) for i in range(2)]
        for at in (first, 4 + first)
    )
    ahead[...] = adaptive(small[0], large[0], line - before)
    back[...] = adaptive(small[1], large[1], line - after)
    forward = lane < 64
    penalty_one = jnp.where(forward, small[0], small[1])

    to = lax.broadcasted_iota(jnp.int32, (256, 256), 0)
    of = lax.broadcasted_iota(jnp.int32, (256, 256), 1)
    order = (of == (to % 8) * TILES + to // 8).astype(jnp.bfloat16)
    for g in range(groups):
        pixels = jnp.concatenate(
            [
                scr[4 * g : 4 * g + 4].reshape(64, 256),
                scr[blocks - 4 * g - 4 : blocks - 4 * g].reshape(64, 256),
            ],
            0,
        )
        turned = lax.dot_general(
            order, pixels, (((1,), (1,)), ((), ())), preferred_element_type=jnp.float32
        )
        costs[g] = turned.astype(jnp.bfloat16)

    mirror = jnp.where(lane < 64, 0, LANES - 1)

    def across_sublanes(lowest):
        for shift in (4, 2, 1):
            lowest = jnp.minimum(lowest, pltpu.roll(lowest, shift, 0))
        return lowest

    def halved(level):
        return [jnp.minimum(level[i], level[i + 1]) for i in range(0, len(level), 2)]

    def lowest_of(level):
        while len(level) > 1:
            level = halved(level)
        return across_sublanes(level[0])

    def costs_at(g, pair):
        both = jnp.dot(costs[g], pick[pair], preferred_element_type=jnp.float32)
        return [both[:, at : at + LANES].reshape(TILES, 8, LANES) for at in (0, LANES)]

    def penalties(g):
        return jnp.where(
            forward,
            jnp.broadcast_to(ahead[pl.ds(g, 1), :], (8, LANES)),
            jnp.broadcast_to(back[pl.ds(groups - 1 - g, 1), :], (8, LANES)),
        )

    def jump_at(g, i):
        return taken(penalties(g), mirror ^ i)

    for i in range(0, AHEAD, 2):
        ready[i], ready[i + 1] = costs_at(0, i // 2)

    def group(g, carried):
        *path, jump = carried
        later = jnp.minimum(g + 1, groups - 1)
        lowest = lowest_of(path)
        for i in range(64):
            if i % 16 == 0:
                path = [x - lowest for x in path]
                lowest = jnp.zeros_like(lowest)
                here = (lane & 63) == 4 * g + i // 16
                for v in range(TILES):
                    starts[v] = jnp.where(here, path[v], starts[v])
            highest = lowest + (jump if i == 0 else jump_at(g, i))
            if i >= AHEAD and i % 2 == 0:
                pair = costs_at(g, i // 2)
            cost = ready[i] if i < AHEAD else pair[i % 2]
            raised = [x + penalty_one for x in path]
            below = jnp.where(sub == 0, FAR, pltpu.roll(raised[-1], 1, 0))
            above = jnp.where(sub == 7, FAR, pltpu.roll(raised[0], 7, 0))
            padded = [below, *raised, above]
            near = [
                jnp.minimum(path[v], jnp.minimum(padded[v], padded[v + 2])) for v in range(TILES)
            ]
            path = [jnp.minimum(near[v], highest) + cost[v] for v in range(TILES)]
            lowest = lowest_of(path)
            if i == 58:
                jump = jump_at(later, 0)
                for k in range(0, AHEAD, 2):
                    ready[k], ready[k + 1] = costs_at(later, k // 2)
        return (*path, jump)

    zero = jnp.zeros((8, LANES), jnp.float32)
    lax.fori_loop(0, groups, group, (zero,) * TILES + (jump_at(0, 0),))
    states[...] = jnp.concatenate([starts[:, s, :] for s in range(8)], 0).T
    for z in range(16):
        block = 2 * z + core if two else z
        fore, rear = ahead[pl.ds(block // 4, 1), :], back[pl.ds(block // 4, 1), :]
        start, end = states[pl.ds(block, 1), :], states[pl.ds(64 + blocks - 1 - block, 1), :]
        out_ref[z, 0:1, :] = jnp.concatenate([start, fore], 1)
        out_ref[z, 1:2, :] = jnp.concatenate([end, rear], 1)


def path_states(blocks, first, two, rows, pick, *sources):
    vmem = pl.BlockSpec(memory_space=pltpu.VMEM)
    return pl.pallas_call(
        partial(path_kernel, blocks, first, two),
        out_shape=jax.ShapeDtypeStruct((16, 2, 384), jnp.float32),
        in_specs=[vmem] * (2 + len(sources)),
        out_specs=vmem,
        scratch_shapes=[
            pltpu.VMEM((blocks, 16, 256), jnp.bfloat16),
            pltpu.VMEM((blocks, LANES), jnp.float32),
            pltpu.VMEM((blocks // 4, LANES), jnp.float32),
            pltpu.VMEM((blocks // 4, LANES), jnp.float32),
            pltpu.VMEM((blocks // 4, 256, LANES), jnp.bfloat16),
            pltpu.VMEM((AHEAD, TILES, 8, LANES), jnp.float32),
            pltpu.VMEM((TILES, 8, LANES), jnp.float32),
            pltpu.VMEM((LANES, 256), jnp.float32),
        ],
        compiler_params=pltpu.CompilerParams(vmem_limit_bytes=12 * 2**20),
        cost_estimate=pl.CostEstimate(
            flops=blocks * 16 * 256 * 128 * 8, bytes_accessed=blocks * 24 * 1024, transcendentals=0
        ),
        name="line_paths",
    )(rows, pick, *sources)


def replay_steps(first, place, rows_ref, entry_ref, line, total, jumps):
    lane = lax.broadcasted_iota(jnp.int32, (16, 256), 1)
    offset = 16 * rows_ref[place : place + 1, :]
    for i in range(2):
        for at in range(16):
            source = jnp.broadcast_to(offset + at, (16, LANES))
            jumps[i, at] = taken(entry_ref[:, i, 256:], source)

    def lowest_of(x):
        return jnp.broadcast_to(jnp.min(x, axis=1, keepdims=True), (16, LANES))

    def wide(x):
        return jnp.concatenate([x, x], 1)

    small = [wide(rows_ref[first + i : first + i + 1, :].astype(jnp.float32)) for i in range(2)]

    def step(j, carried):
        done = []
        for i, at in enumerate((j, 15 - j)):
            path, lowest = carried[i]
            cost = line[at]
            below = jnp.where(lane == 0, FAR, pltpu.roll(path, 1, 1))
            above = jnp.where(lane == 255, FAR, pltpu.roll(path, 255, 1))
            near = jnp.minimum(path, jnp.minimum(below, above) + small[i]) + cost
            highest = lowest + jumps[i, at]
            path = jnp.minimum(near, wide(highest) + cost)
            total[at] += path - wide(lowest)
            lowest = jnp.minimum(lowest_of(near), highest + lowest_of(cost))
            done.append((path, lowest))
        return tuple(done)

    paths = [entry_ref[:, i, 0:256] for i in range(2)]
    lax.fori_loop(0, 16, step, tuple((path, lowest_of(path)) for path in paths), unroll=UNROLL)


def columns_replay_kernel(rows_ref, entry_ref, cost_ref, sum_ref, line_ref, line, total, jumps):
    cost = cost_ref[...].astype(jnp.float32)
    line[...] = cost
    total[...] = jnp.zeros_like(total)
    replay_steps(2, 9, rows_ref, entry_ref, line, total, jumps)
    sum_ref[...] = jnp.swapaxes(total[...], 0, 1)
    line_ref[...] = jnp.swapaxes(cost, 0, 1)


def lines_replay_kernel(rows_ref, entry_ref, sum_ref, line_ref, out_ref, total, jumps):
    total[...] = sum_ref[...]
    replay_steps(0, 8, rows_ref, entry_ref, line_ref, total, jumps)
    out_ref[...] = jnp.swapaxes(total[...], 0, 1) * OUT_SCALE


def replay(kernel, outs, *operands):
    block = jax.ShapeDtypeStruct((16, 16, 256), jnp.float32)
    vmem = pl.BlockSpec(memory_space=pltpu.VMEM)
    return pl.pallas_call(
        kernel,
        out_shape=[block] * outs,
        in_specs=[vmem] * len(operands),
        out_specs=[vmem] * outs,
        scratch_shapes=[pltpu.VMEM(block.shape, block.dtype)] * outs
        + [pltpu.VMEM((2, 16, 16, LANES), jnp.float32)],
        cost_estimate=pl.CostEstimate(
            flops=2 * 65536 * 100, bytes_accessed=2**20, transcendentals=0
        ),
        compiler_params=pltpu.CompilerParams(vmem_limit_bytes=4 * 2**20),
        name="block_paths",
    )(*operands)


def column_message_kernel(cost_hbm, image_hbm, out_ref, cost_ref, image_ref, cost_sem, image_sem):
    cost_copy = pltpu.make_async_copy(cost_hbm, cost_ref, cost_sem)
    image_copy = pltpu.make_async_copy(image_hbm, image_ref, image_sem)
    cost_copy.start()
    image_copy.start()
    cost_copy.wait()
    image_copy.wait()
    crossed = jnp.swapaxes(cost_ref[...].astype(jnp.float32), 0, 1)
    out_ref[:, 0:16, :] = crossed[:, :, 0:LANES]
    out_ref[:, 16:32, :] = crossed[:, :, LANES:]
    row = lax.broadcasted_iota(jnp.int32, (16, LANES), 0)
    lane = lax.broadcasted_iota(jnp.int32, (16, LANES), 1)
    image = image_ref[...]
    for c in range(16):
        column = jnp.where(lane % 16 == row, image[:, c : c + 1], 0.0)
        line = jnp.sum(column, axis=0, keepdims=True)
        out_ref[c, 32:40, :] = jnp.broadcast_to(line, (8, LANES))


def column_message(cost, image):
    return pl.pallas_call(
        column_message_kernel,
        out_shape=jax.ShapeDtypeStruct((16, ROWS, LANES), jnp.float32),
        in_specs=[pl.BlockSpec(memory_space=pltpu.HBM)] * 2,
        out_specs=pl.BlockSpec(memory_space=pltpu.VMEM),
        scratch_shapes=[
            pltpu.VMEM((16, 16, 256), jnp.int32),
            pltpu.VMEM((16, 16), jnp.float32),
            pltpu.SemaphoreType.DMA,
            pltpu.SemaphoreType.DMA,
        ],
        compiler_params=pltpu.CompilerParams(vmem_limit_bytes=56 * 2**20),
        name="column_message",
    )(cost, image)


def message(cost, image):
    wide = jnp.tile(image, (1, LANES // 16))[:, None, :]
    empty = jnp.zeros((16, ROWS - 33, LANES), jnp.float32)
    cost = cost.astype(jnp.float32)
    return jnp.concatenate([cost[:, :, :LANES], cost[:, :, LANES:], wide, empty], 1)


def after_kernel(value_ref, earlier_ref, out_ref):
    out_ref[...] = value_ref[...]


def pass_kernel(value_ref, earlier_ref, out_ref):
    pass


def passed_after(value, earlier):
    return pl.pallas_call(
        pass_kernel,
        out_shape=jax.ShapeDtypeStruct(value.shape, value.dtype),
        in_specs=[pl.BlockSpec(memory_space=pl.ANY), pl.BlockSpec(memory_space=pltpu.VMEM)],
        out_specs=pl.BlockSpec(memory_space=pl.ANY),
        input_output_aliases={0: 0},
        compiler_params=pltpu.CompilerParams(vmem_limit_bytes=2 * 2**20),
        name="passed_after",
    )(value, earlier)


def after(value, earlier):
    vmem = pl.BlockSpec(memory_space=pltpu.VMEM)
    return pl.pallas_call(
        after_kernel,
        out_shape=jax.ShapeDtypeStruct(value.shape, value.dtype),
        in_specs=[vmem, pl.BlockSpec(memory_space=pl.ANY)],
        out_specs=vmem,
        compiler_params=pltpu.CompilerParams(vmem_limit_bytes=2 * 2**20),
        name="after",
    )(value, earlier)


def on_device(cost_volume, left_image, p_small, p_large):
    index_x, index_y = lax.axis_index("gx"), lax.axis_index("gy")
    here = jnp.stack([index_x % 4, index_y % 4]).astype(jnp.int32)
    numbers = jnp.concatenate([p_small, p_large, here])
    rows = jnp.broadcast_to(jnp.pad(numbers, (0, 6))[:, None], (16, LANES))
    pair, pixel, path = (
        lax.broadcasted_iota(jnp.int32, (32, LANES, 2 * LANES), i) for i in range(3)
    )
    step = 2 * pair + path // LANES
    pick = (pixel == jnp.where(path % LANES < 64, step, LANES - 1 - step)).astype(jnp.bfloat16)
    chips = [[2 * z + c for z in range(16)] for c in range(2)]
    swap = [(i, i ^ 1) for i in range(32)]

    columns = column_message(cost_volume, left_image)
    lines = message(cost_volume, left_image)
    columns = lax.all_to_all(columns, "gy", 0, 0)
    lines = passed_after(lines, columns)
    lines = lax.all_to_all(lines, "gx", 0, 0, axis_index_groups=chips)
    entry_y = path_states(16, 2, False, rows, pick, columns)
    lines = after(lines, entry_y)
    others = lax.ppermute(lines, "gx", swap)

    entry_y = lax.all_to_all(entry_y, "gy", 0, 0)
    entry_x = path_states(32, 0, True, rows, pick, lines, others)
    entry_x = lax.all_to_all(entry_x, "gx", 0, 0, axis_index_groups=chips)

    total, line = replay(columns_replay_kernel, 2, rows, entry_y, cost_volume)
    return replay(lines_replay_kernel, 1, rows, entry_x, total, line)[0]


def solution(mesh):
    in_specs = (P("gy", "gx", None), P("gy", "gx"), P(), P())
    out_specs = P("gy", "gx", None)
    return jax.shard_map(
        on_device, mesh=mesh, in_specs=in_specs, out_specs=out_specs, check_vma=False
    )
```

```python
from functools import partial

import jax
import jax.numpy as jnp
from jax import lax
from jax.experimental import pallas as pl
from jax.experimental.pallas import tpu as pltpu
from jax.sharding import PartitionSpec as P

FAR = 1e30
GRADIENT_GAIN = 4.0
OUT_SCALE = 1.0 / 256.0
LANES = 128
TILES = 32
UNROLL = 4
AHEAD = 4
ROWS = 40


def adaptive(penalty_one, penalty_two, step_diff):
    return penalty_one + (penalty_two - penalty_one) / (1.0 + GRADIENT_GAIN * jnp.abs(step_diff))


def taken(values, lanes):
    return jnp.take_along_axis(values, lanes, axis=1, mode="promise_in_bounds")


def gather_costs(blocks, two, core, sources, scr, img):
    def fetch(z, nothing):
        for which, source in enumerate(sources):
            if two:
                place = 2 * z + core if which == 0 else 2 * z + 1 - core
            else:
                place = z
            scr[place, :, 0:LANES] = source[z, 0:16, :].astype(jnp.bfloat16)
            scr[place, :, LANES:] = source[z, 16:32, :].astype(jnp.bfloat16)
            img[pl.ds(place, 1), :] = source[z, 32:33, :]
        return nothing

    lax.fori_loop(0, 16, fetch, 0, unroll=4)


def path_kernel(blocks, first, two, rows_ref, pick, *refs):
    sources, (out_ref, scr, img, ahead, back, costs, ready, starts, states) = refs[:-9], refs[-9:]
    groups = blocks // 4
    lane = lax.broadcasted_iota(jnp.int32, (8, LANES), 1)
    sub = lax.broadcasted_iota(jnp.int32, (8, LANES), 0)
    core = lax.axis_index("gx") % 2 if two else 0
    gather_costs(blocks, two, core, sources, scr, img)

    place, row = lane[:groups] % 64, sub[:groups]
    line = img[pl.ds(0, groups, stride=4), :]
    for k in range(1, 4):
        line = jnp.where(place // 16 == k, img[pl.ds(k, groups, stride=4), :], line)
    before = pltpu.roll(line, 1, 1)
    wrapped = jnp.concatenate([before[groups - 1 :], before[: groups - 1]], 0)
    before = jnp.where(place == 0, jnp.where(row == 0, 0.0, wrapped), before)
    after = pltpu.roll(line, LANES - 1, 1)
    wrapped = jnp.concatenate([after[1:], after[:1]], 0)
    after = jnp.where(place == 63, jnp.where(row == groups - 1, 0.0, wrapped), after)
    small, large = (
        [rows_ref[at + i : at + i + 1, :].astype(jnp.float32) for i in range(2)]
        for at in (first, 4 + first)
    )
    ahead[...] = adaptive(small[0], large[0], line - before)
    back[...] = adaptive(small[1], large[1], line - after)
    forward = lane < 64
    penalty_one = jnp.where(forward, small[0], small[1])

    to = lax.broadcasted_iota(jnp.int32, (256, 256), 0)
    of = lax.broadcasted_iota(jnp.int32, (256, 256), 1)
    order = (of == (to % 8) * TILES + to // 8).astype(jnp.bfloat16)
    for g in range(groups):
        pixels = jnp.concatenate(
            [
                scr[4 * g : 4 * g + 4].reshape(64, 256),
                scr[blocks - 4 * g - 4 : blocks - 4 * g].reshape(64, 256),
            ],
            0,
        )
        turned = lax.dot_general(
            order, pixels, (((1,), (1,)), ((), ())), preferred_element_type=jnp.float32
        )
        costs[g] = turned.astype(jnp.bfloat16)

    mirror = jnp.where(lane < 64, 0, LANES - 1)

    def across_sublanes(lowest):
        for shift in (4, 2, 1):
            lowest = jnp.minimum(lowest, pltpu.roll(lowest, shift, 0))
        return lowest

    def halved(level):
        return [jnp.minimum(level[i], level[i + 1]) for i in range(0, len(level), 2)]

    def lowest_of(level):
        while len(level) > 1:
            level = halved(level)
        return across_sublanes(level[0])

    def costs_at(g, pair):
        both = jnp.dot(costs[g], pick[pair], preferred_element_type=jnp.float32)
        return [both[:, at : at + LANES].reshape(TILES, 8, LANES) for at in (0, LANES)]

    def penalties(g):
        return jnp.where(
            forward,
            jnp.broadcast_to(ahead[pl.ds(g, 1), :], (8, LANES)),
            jnp.broadcast_to(back[pl.ds(groups - 1 - g, 1), :], (8, LANES)),
        )

    def jump_at(g, i):
        return taken(penalties(g), mirror ^ i)

    for i in range(0, AHEAD, 2):
        ready[i], ready[i + 1] = costs_at(0, i // 2)

    def group(g, carried):
        *path, jump = carried
        later = jnp.minimum(g + 1, groups - 1)
        lowest = lowest_of(path)
        for i in range(64):
            if i % 16 == 0:
                path = [x - lowest for x in path]
                lowest = jnp.zeros_like(lowest)
                here = (lane & 63) == 4 * g + i // 16
                for v in range(TILES):
                    starts[v] = jnp.where(here, path[v], starts[v])
            highest = lowest + (jump if i == 0 else jump_at(g, i))
            if i >= AHEAD and i % 2 == 0:
                pair = costs_at(g, i // 2)
            cost = ready[i] if i < AHEAD else pair[i % 2]
            raised = [x + penalty_one for x in path]
            below = jnp.where(sub == 0, FAR, pltpu.roll(raised[-1], 1, 0))
            above = jnp.where(sub == 7, FAR, pltpu.roll(raised[0], 7, 0))
            padded = [below, *raised, above]
            near = [
                jnp.minimum(path[v], jnp.minimum(padded[v], padded[v + 2])) for v in range(TILES)
            ]
            path = [jnp.minimum(near[v], highest) + cost[v] for v in range(TILES)]
            lowest = lowest_of(path)
            if i == 58:
                jump = jump_at(later, 0)
                for k in range(0, AHEAD, 2):
                    ready[k], ready[k + 1] = costs_at(later, k // 2)
        return (*path, jump)

    zero = jnp.zeros((8, LANES), jnp.float32)
    lax.fori_loop(0, groups, group, (zero,) * TILES + (jump_at(0, 0),))
    states[...] = jnp.concatenate([starts[:, s, :] for s in range(8)], 0).T
    for z in range(16):
        block = 2 * z + core if two else z
        fore, rear = ahead[pl.ds(block // 4, 1), :], back[pl.ds(block // 4, 1), :]
        start, end = states[pl.ds(block, 1), :], states[pl.ds(64 + blocks - 1 - block, 1), :]
        out_ref[z, 0:1, :] = jnp.concatenate([start, fore], 1)
        out_ref[z, 1:2, :] = jnp.concatenate([end, rear], 1)


def path_states(blocks, first, two, rows, pick, *sources):
    vmem = pl.BlockSpec(memory_space=pltpu.VMEM)
    return pl.pallas_call(
        partial(path_kernel, blocks, first, two),
        out_shape=jax.ShapeDtypeStruct((16, 2, 384), jnp.float32),
        in_specs=[vmem] * (2 + len(sources)),
        out_specs=vmem,
        scratch_shapes=[
            pltpu.VMEM((blocks, 16, 256), jnp.bfloat16),
            pltpu.VMEM((32, LANES), jnp.float32),
            pltpu.VMEM((blocks // 4, LANES), jnp.float32),
            pltpu.VMEM((blocks // 4, LANES), jnp.float32),
            pltpu.VMEM((blocks // 4, 256, LANES), jnp.bfloat16),
            pltpu.VMEM((AHEAD, TILES, 8, LANES), jnp.float32),
            pltpu.VMEM((TILES, 8, LANES), jnp.float32),
            pltpu.VMEM((LANES, 256), jnp.float32),
        ],
        compiler_params=pltpu.CompilerParams(vmem_limit_bytes=12 * 2**20),
        cost_estimate=pl.CostEstimate(
            flops=blocks * 16 * 256 * 128 * 8, bytes_accessed=blocks * 24 * 1024, transcendentals=0
        ),
        name="line_paths",
    )(rows, pick, *sources)


def replay_steps(first, place, rows_ref, entry_ref, line, total, jumps):
    lane = lax.broadcasted_iota(jnp.int32, (16, 256), 1)
    offset = 16 * rows_ref[place : place + 1, :]
    for i in range(2):
        for at in range(16):
            source = jnp.broadcast_to(offset + at, (16, LANES))
            jumps[i, at] = taken(entry_ref[:, i, 256:], source)

    def lowest_of(x):
        return jnp.broadcast_to(jnp.min(x, axis=1, keepdims=True), (16, LANES))

    def wide(x):
        return jnp.concatenate([x, x], 1)

    small = [wide(rows_ref[first + i : first + i + 1, :].astype(jnp.float32)) for i in range(2)]

    def step(j, carried):
        done = []
        for i, at in enumerate((j, 15 - j)):
            path, lowest = carried[i]
            cost = line[at]
            below = jnp.where(lane == 0, FAR, pltpu.roll(path, 1, 1))
            above = jnp.where(lane == 255, FAR, pltpu.roll(path, 255, 1))
            near = jnp.minimum(path, jnp.minimum(below, above) + small[i]) + cost
            highest = lowest + jumps[i, at]
            path = jnp.minimum(near, wide(highest) + cost)
            total[at] += path - wide(lowest)
            lowest = jnp.minimum(lowest_of(near), highest + lowest_of(cost))
            done.append((path, lowest))
        return tuple(done)

    paths = [entry_ref[:, i, 0:256] for i in range(2)]
    lax.fori_loop(0, 16, step, tuple((path, lowest_of(path)) for path in paths), unroll=UNROLL)


def columns_replay_kernel(rows_ref, entry_ref, cost_ref, sum_ref, line_ref, line, total, jumps):
    cost = cost_ref[...].astype(jnp.float32)
    line[...] = cost
    total[...] = jnp.zeros_like(total)
    replay_steps(2, 9, rows_ref, entry_ref, line, total, jumps)
    sum_ref[...] = jnp.swapaxes(total[...], 0, 1)
    line_ref[...] = jnp.swapaxes(cost, 0, 1)


def lines_replay_kernel(rows_ref, entry_ref, sum_ref, line_ref, out_ref, total, jumps):
    total[...] = sum_ref[...]
    replay_steps(0, 8, rows_ref, entry_ref, line_ref, total, jumps)
    out_ref[...] = jnp.swapaxes(total[...], 0, 1) * OUT_SCALE


def replay(kernel, outs, *operands):
    block = jax.ShapeDtypeStruct((16, 16, 256), jnp.float32)
    vmem = pl.BlockSpec(memory_space=pltpu.VMEM)
    return pl.pallas_call(
        kernel,
        out_shape=[block] * outs,
        in_specs=[vmem] * len(operands),
        out_specs=[vmem] * outs,
        scratch_shapes=[pltpu.VMEM(block.shape, block.dtype)] * outs
        + [pltpu.VMEM((2, 16, 16, LANES), jnp.float32)],
        cost_estimate=pl.CostEstimate(
            flops=2 * 65536 * 100, bytes_accessed=2**20, transcendentals=0
        ),
        compiler_params=pltpu.CompilerParams(vmem_limit_bytes=4 * 2**20),
        name="block_paths",
    )(*operands)


def column_message_kernel(cost_hbm, image_hbm, out_ref, cost_ref, image_ref, cost_sem, image_sem):
    cost_copy = pltpu.make_async_copy(cost_hbm, cost_ref, cost_sem)
    image_copy = pltpu.make_async_copy(image_hbm, image_ref, image_sem)
    cost_copy.start()
    image_copy.start()
    cost_copy.wait()
    image_copy.wait()
    crossed = jnp.swapaxes(cost_ref[...].astype(jnp.float32), 0, 1)
    out_ref[:, 0:16, :] = crossed[:, :, 0:LANES]
    out_ref[:, 16:32, :] = crossed[:, :, LANES:]
    row = lax.broadcasted_iota(jnp.int32, (16, LANES), 0)
    lane = lax.broadcasted_iota(jnp.int32, (16, LANES), 1)
    image = image_ref[...]
    for c in range(16):
        column = jnp.where(lane % 16 == row, image[:, c : c + 1], 0.0)
        line = jnp.sum(column, axis=0, keepdims=True)
        out_ref[c, 32:40, :] = jnp.broadcast_to(line, (8, LANES))


def column_message(cost, image):
    return pl.pallas_call(
        column_message_kernel,
        out_shape=jax.ShapeDtypeStruct((16, ROWS, LANES), jnp.float32),
        in_specs=[pl.BlockSpec(memory_space=pltpu.HBM)] * 2,
        out_specs=pl.BlockSpec(memory_space=pltpu.VMEM),
        scratch_shapes=[
            pltpu.VMEM((16, 16, 256), jnp.int32),
            pltpu.VMEM((16, 16), jnp.float32),
            pltpu.SemaphoreType.DMA,
            pltpu.SemaphoreType.DMA,
        ],
        compiler_params=pltpu.CompilerParams(vmem_limit_bytes=56 * 2**20),
        name="column_message",
    )(cost, image)


def message(cost, image):
    wide = jnp.tile(image, (1, LANES // 16))[:, None, :]
    empty = jnp.zeros((16, ROWS - 33, LANES), jnp.float32)
    cost = cost.astype(jnp.float32)
    return jnp.concatenate([cost[:, :, :LANES], cost[:, :, LANES:], wide, empty], 1)


def after_kernel(value_ref, earlier_ref, out_ref):
    out_ref[...] = value_ref[...]


def pass_kernel(value_ref, earlier_ref, out_ref):
    pass


def passed_after(value, earlier):
    return pl.pallas_call(
        pass_kernel,
        out_shape=jax.ShapeDtypeStruct(value.shape, value.dtype),
        in_specs=[pl.BlockSpec(memory_space=pl.ANY), pl.BlockSpec(memory_space=pltpu.VMEM)],
        out_specs=pl.BlockSpec(memory_space=pl.ANY),
        input_output_aliases={0: 0},
        compiler_params=pltpu.CompilerParams(vmem_limit_bytes=2 * 2**20),
        name="passed_after",
    )(value, earlier)


def after(value, earlier):
    vmem = pl.BlockSpec(memory_space=pltpu.VMEM)
    return pl.pallas_call(
        after_kernel,
        out_shape=jax.ShapeDtypeStruct(value.shape, value.dtype),
        in_specs=[vmem, pl.BlockSpec(memory_space=pl.ANY)],
        out_specs=vmem,
        compiler_params=pltpu.CompilerParams(vmem_limit_bytes=2 * 2**20),
        name="after",
    )(value, earlier)


def on_device(cost_volume, left_image, p_small, p_large):
    index_x, index_y = lax.axis_index("gx"), lax.axis_index("gy")
    here = jnp.stack([index_x % 4, index_y % 4]).astype(jnp.int32)
    numbers = jnp.concatenate([p_small, p_large, here])
    rows = jnp.broadcast_to(jnp.pad(numbers, (0, 6))[:, None], (16, LANES))
    pair, pixel, path = (
        lax.broadcasted_iota(jnp.int32, (32, LANES, 2 * LANES), i) for i in range(3)
    )
    step = 2 * pair + path // LANES
    pick = (pixel == jnp.where(path % LANES < 64, step, LANES - 1 - step)).astype(jnp.bfloat16)
    chips = [[2 * z + c for z in range(16)] for c in range(2)]
    swap = [(i, i ^ 1) for i in range(32)]

    columns = column_message(cost_volume, left_image)
    lines = message(cost_volume, left_image)
    columns = lax.all_to_all(columns, "gy", 0, 0)
    lines = passed_after(lines, columns)
    lines = lax.all_to_all(lines, "gx", 0, 0, axis_index_groups=chips)
    entry_y = path_states(16, 2, False, rows, pick, columns)
    lines = after(lines, entry_y)
    others = lax.ppermute(lines, "gx", swap)

    entry_y = lax.all_to_all(entry_y, "gy", 0, 0)
    entry_x = path_states(32, 0, True, rows, pick, lines, others)
    entry_x = lax.all_to_all(entry_x, "gx", 0, 0, axis_index_groups=chips)

    total, line = replay(columns_replay_kernel, 2, rows, entry_y, cost_volume)
    return replay(lines_replay_kernel, 1, rows, entry_x, total, line)[0]


def solution(mesh):
    in_specs = (P("gy", "gx", None), P("gy", "gx"), P(), P())
    out_specs = P("gy", "gx", None)
    return jax.shard_map(
        on_device, mesh=mesh, in_specs=in_specs, out_specs=out_specs, check_vma=False
    )
```

```python
from functools import partial

import jax
import jax.numpy as jnp
from jax import lax
from jax.experimental import pallas as pl
from jax.experimental.pallas import tpu as pltpu
from jax.sharding import PartitionSpec as P

FAR = 1e30
GRADIENT_GAIN = 4.0
OUT_SCALE = 1.0 / 256.0
LANES = 128
TILES = 32
UNROLL = 4
AHEAD = 4
ROWS = 40


def adaptive(penalty_one, penalty_two, step_diff):
    return penalty_one + (penalty_two - penalty_one) / (1.0 + GRADIENT_GAIN * jnp.abs(step_diff))


def taken(values, lanes):
    return jnp.take_along_axis(values, lanes, axis=1, mode="promise_in_bounds")


def gather_costs(blocks, two, core, sources, scr, img):
    def fetch(z, nothing):
        for which, source in enumerate(sources):
            if two:
                place = 2 * z + core if which == 0 else 2 * z + 1 - core
            else:
                place = z
            scr[place, :, 0:LANES] = source[z, 0:16, :].astype(jnp.bfloat16)
            scr[place, :, LANES:] = source[z, 16:32, :].astype(jnp.bfloat16)
            img[pl.ds(place, 1), :] = source[z, 32:33, :]
        return nothing

    lax.fori_loop(0, 16, fetch, 0, unroll=4)


def path_kernel(blocks, first, two, rows_ref, pick, *refs):
    sources, (out_ref, scr, img, ahead, back, costs, ready, starts, states) = refs[:-9], refs[-9:]
    groups = blocks // 4
    lane = lax.broadcasted_iota(jnp.int32, (8, LANES), 1)
    sub = lax.broadcasted_iota(jnp.int32, (8, LANES), 0)
    core = lax.axis_index("gx") % 2 if two else 0
    gather_costs(blocks, two, core, sources, scr, img)

    place, row = lane[:groups] % 64, sub[:groups]
    line = img[pl.ds(0, groups, stride=4), :]
    for k in range(1, 4):
        line = jnp.where(place // 16 == k, img[pl.ds(k, groups, stride=4), :], line)
    before = pltpu.roll(line, 1, 1)
    wrapped = jnp.concatenate([before[groups - 1 :], before[: groups - 1]], 0)
    before = jnp.where(place == 0, jnp.where(row == 0, 0.0, wrapped), before)
    after = pltpu.roll(line, LANES - 1, 1)
    wrapped = jnp.concatenate([after[1:], after[:1]], 0)
    after = jnp.where(place == 63, jnp.where(row == groups - 1, 0.0, wrapped), after)
    small, large = (
        [rows_ref[at + i : at + i + 1, :].astype(jnp.float32) for i in range(2)]
        for at in (first, 4 + first)
    )
    ahead[...] = adaptive(small[0], large[0], line - before)
    back[...] = adaptive(small[1], large[1], line - after)
    forward = lane < 64
    penalty_one = jnp.where(forward, small[0], small[1])

    to = lax.broadcasted_iota(jnp.int32, (256, 256), 0)
    of = lax.broadcasted_iota(jnp.int32, (256, 256), 1)
    order = (of == (to % 8) * TILES + to // 8).astype(jnp.bfloat16)
    def turn(g, nothing):
        pixels = jnp.concatenate(
            [
                scr[pl.ds(4 * g, 4)].reshape(64, 256),
                scr[pl.ds(blocks - 4 - 4 * g, 4)].reshape(64, 256),
            ],
            0,
        )
        turned = lax.dot_general(
            order, pixels, (((1,), (1,)), ((), ())), preferred_element_type=jnp.float32
        )
        costs[g] = turned.astype(jnp.bfloat16)
        return nothing

    lax.fori_loop(0, groups, turn, 0, unroll=4)

    mirror = jnp.where(lane < 64, 0, LANES - 1)

    def across_sublanes(lowest):
        for shift in (4, 2, 1):
            lowest = jnp.minimum(lowest, pltpu.roll(lowest, shift, 0))
        return lowest

    def halved(level):
        return [jnp.minimum(level[i], level[i + 1]) for i in range(0, len(level), 2)]

    def lowest_of(level):
        while len(level) > 1:
            level = halved(level)
        return across_sublanes(level[0])

    def costs_at(g, pair):
        both = jnp.dot(costs[g], pick[pair], preferred_element_type=jnp.float32)
        return [both[:, at : at + LANES].reshape(TILES, 8, LANES) for at in (0, LANES)]

    def penalties(g):
        return jnp.where(
            forward,
            jnp.broadcast_to(ahead[pl.ds(g, 1), :], (8, LANES)),
            jnp.broadcast_to(back[pl.ds(groups - 1 - g, 1), :], (8, LANES)),
        )

    def jump_at(g, i):
        return taken(penalties(g), mirror ^ i)

    for i in range(0, AHEAD, 2):
        ready[i], ready[i + 1] = costs_at(0, i // 2)

    def group(g, carried):
        *path, jump = carried
        later = jnp.minimum(g + 1, groups - 1)
        lowest = lowest_of(path)
        for i in range(64):
            if i % 16 == 0:
                path = [x - lowest for x in path]
                lowest = jnp.zeros_like(lowest)
                here = (lane & 63) == 4 * g + i // 16
                for v in range(TILES):
                    starts[v] = jnp.where(here, path[v], starts[v])
            highest = lowest + (jump if i == 0 else jump_at(g, i))
            if i >= AHEAD and i % 2 == 0:
                pair = costs_at(g, i // 2)
            cost = ready[i] if i < AHEAD else pair[i % 2]
            raised = [x + penalty_one for x in path]
            below = jnp.where(sub == 0, FAR, pltpu.roll(raised[-1], 1, 0))
            above = jnp.where(sub == 7, FAR, pltpu.roll(raised[0], 7, 0))
            padded = [below, *raised, above]
            near = [
                jnp.minimum(path[v], jnp.minimum(padded[v], padded[v + 2])) for v in range(TILES)
            ]
            path = [jnp.minimum(near[v], highest) + cost[v] for v in range(TILES)]
            lowest = lowest_of(path)
            if i == 58:
                jump = jump_at(later, 0)
                for k in range(0, AHEAD, 2):
                    ready[k], ready[k + 1] = costs_at(later, k // 2)
        return (*path, jump)

    zero = jnp.zeros((8, LANES), jnp.float32)
    lax.fori_loop(0, groups, group, (zero,) * TILES + (jump_at(0, 0),))
    states[...] = jnp.concatenate([starts[:, s, :] for s in range(8)], 0).T
    def send(z, nothing):
        block = 2 * z + core if two else z
        fore, rear = ahead[pl.ds(block >> 2, 1), :], back[pl.ds(block >> 2, 1), :]
        start, end = states[pl.ds(block, 1), :], states[pl.ds(64 + blocks - 1 - block, 1), :]
        out_ref[z, 0:1, :] = jnp.concatenate([start, fore], 1)
        out_ref[z, 1:2, :] = jnp.concatenate([end, rear], 1)
        return nothing

    lax.fori_loop(0, 16, send, 0, unroll=4)


def path_states(blocks, first, two, rows, pick, *sources):
    vmem = pl.BlockSpec(memory_space=pltpu.VMEM)
    return pl.pallas_call(
        partial(path_kernel, blocks, first, two),
        out_shape=jax.ShapeDtypeStruct((16, 2, 384), jnp.float32),
        in_specs=[vmem] * (2 + len(sources)),
        out_specs=vmem,
        scratch_shapes=[
            pltpu.VMEM((blocks, 16, 256), jnp.bfloat16),
            pltpu.VMEM((32, LANES), jnp.float32),
            pltpu.VMEM((blocks // 4, LANES), jnp.float32),
            pltpu.VMEM((blocks // 4, LANES), jnp.float32),
            pltpu.VMEM((blocks // 4, 256, LANES), jnp.bfloat16),
            pltpu.VMEM((AHEAD, TILES, 8, LANES), jnp.float32),
            pltpu.VMEM((TILES, 8, LANES), jnp.float32),
            pltpu.VMEM((LANES, 256), jnp.float32),
        ],
        compiler_params=pltpu.CompilerParams(vmem_limit_bytes=12 * 2**20),
        cost_estimate=pl.CostEstimate(
            flops=blocks * 16 * 256 * 128 * 8, bytes_accessed=blocks * 24 * 1024, transcendentals=0
        ),
        name="line_paths",
    )(rows, pick, *sources)


def replay_steps(first, place, rows_ref, entry_ref, line, total, jumps):
    lane = lax.broadcasted_iota(jnp.int32, (16, 256), 1)
    offset = 16 * rows_ref[place : place + 1, :]
    for i in range(2):
        for at in range(16):
            source = jnp.broadcast_to(offset + at, (16, LANES))
            jumps[i, at] = taken(entry_ref[:, i, 256:], source)

    def lowest_of(x):
        return jnp.broadcast_to(jnp.min(x, axis=1, keepdims=True), (16, LANES))

    def wide(x):
        return jnp.concatenate([x, x], 1)

    small = [wide(rows_ref[first + i : first + i + 1, :].astype(jnp.float32)) for i in range(2)]

    def step(j, carried):
        done = []
        for i, at in enumerate((j, 15 - j)):
            path, lowest = carried[i]
            cost = line[at]
            below = jnp.where(lane == 0, FAR, pltpu.roll(path, 1, 1))
            above = jnp.where(lane == 255, FAR, pltpu.roll(path, 255, 1))
            near = jnp.minimum(path, jnp.minimum(below, above) + small[i]) + cost
            highest = lowest + jumps[i, at]
            path = jnp.minimum(near, wide(highest) + cost)
            total[at] += path - wide(lowest)
            lowest = jnp.minimum(lowest_of(near), highest + lowest_of(cost))
            done.append((path, lowest))
        return tuple(done)

    paths = [entry_ref[:, i, 0:256] for i in range(2)]
    lax.fori_loop(0, 16, step, tuple((path, lowest_of(path)) for path in paths), unroll=UNROLL)


def columns_replay_kernel(rows_ref, entry_ref, cost_ref, sum_ref, line_ref, line, total, jumps):
    cost = cost_ref[...].astype(jnp.float32)
    line[...] = cost
    total[...] = jnp.zeros_like(total)
    replay_steps(2, 9, rows_ref, entry_ref, line, total, jumps)
    sum_ref[...] = jnp.swapaxes(total[...], 0, 1)
    line_ref[...] = jnp.swapaxes(cost, 0, 1)


def lines_replay_kernel(rows_ref, entry_ref, sum_ref, line_ref, out_ref, total, jumps):
    total[...] = sum_ref[...]
    replay_steps(0, 8, rows_ref, entry_ref, line_ref, total, jumps)
    out_ref[...] = jnp.swapaxes(total[...], 0, 1) * OUT_SCALE


def replay(kernel, outs, *operands):
    block = jax.ShapeDtypeStruct((16, 16, 256), jnp.float32)
    vmem = pl.BlockSpec(memory_space=pltpu.VMEM)
    return pl.pallas_call(
        kernel,
        out_shape=[block] * outs,
        in_specs=[vmem] * len(operands),
        out_specs=[vmem] * outs,
        scratch_shapes=[pltpu.VMEM(block.shape, block.dtype)] * outs
        + [pltpu.VMEM((2, 16, 16, LANES), jnp.float32)],
        cost_estimate=pl.CostEstimate(
            flops=2 * 65536 * 100, bytes_accessed=2**20, transcendentals=0
        ),
        compiler_params=pltpu.CompilerParams(vmem_limit_bytes=4 * 2**20),
        name="block_paths",
    )(*operands)


def column_message_kernel(cost_hbm, image_hbm, out_ref, cost_ref, image_ref, cost_sem, image_sem):
    cost_copy = pltpu.make_async_copy(cost_hbm, cost_ref, cost_sem)
    image_copy = pltpu.make_async_copy(image_hbm, image_ref, image_sem)
    cost_copy.start()
    image_copy.start()
    cost_copy.wait()
    image_copy.wait()
    crossed = jnp.swapaxes(cost_ref[...].astype(jnp.float32), 0, 1)
    out_ref[:, 0:16, :] = crossed[:, :, 0:LANES]
    out_ref[:, 16:32, :] = crossed[:, :, LANES:]
    row = lax.broadcasted_iota(jnp.int32, (16, LANES), 0)
    lane = lax.broadcasted_iota(jnp.int32, (16, LANES), 1)
    image = image_ref[...]
    for c in range(16):
        column = jnp.where(lane % 16 == row, image[:, c : c + 1], 0.0)
        line = jnp.sum(column, axis=0, keepdims=True)
        out_ref[c, 32:40, :] = jnp.broadcast_to(line, (8, LANES))


def column_message(cost, image):
    return pl.pallas_call(
        column_message_kernel,
        out_shape=jax.ShapeDtypeStruct((16, ROWS, LANES), jnp.float32),
        in_specs=[pl.BlockSpec(memory_space=pltpu.HBM)] * 2,
        out_specs=pl.BlockSpec(memory_space=pltpu.VMEM),
        scratch_shapes=[
            pltpu.VMEM((16, 16, 256), jnp.int32),
            pltpu.VMEM((16, 16), jnp.float32),
            pltpu.SemaphoreType.DMA,
            pltpu.SemaphoreType.DMA,
        ],
        compiler_params=pltpu.CompilerParams(vmem_limit_bytes=56 * 2**20),
        name="column_message",
    )(cost, image)


def message(cost, image):
    wide = jnp.tile(image, (1, LANES // 16))[:, None, :]
    empty = jnp.zeros((16, ROWS - 33, LANES), jnp.float32)
    cost = cost.astype(jnp.float32)
    return jnp.concatenate([cost[:, :, :LANES], cost[:, :, LANES:], wide, empty], 1)


def after_kernel(value_ref, earlier_ref, out_ref):
    out_ref[...] = value_ref[...]


def pass_kernel(value_ref, earlier_ref, out_ref):
    pass


def passed_after(value, earlier):
    return pl.pallas_call(
        pass_kernel,
        out_shape=jax.ShapeDtypeStruct(value.shape, value.dtype),
        in_specs=[pl.BlockSpec(memory_space=pl.ANY), pl.BlockSpec(memory_space=pltpu.VMEM)],
        out_specs=pl.BlockSpec(memory_space=pl.ANY),
        input_output_aliases={0: 0},
        compiler_params=pltpu.CompilerParams(vmem_limit_bytes=2 * 2**20),
        name="passed_after",
    )(value, earlier)


def after(value, earlier):
    vmem = pl.BlockSpec(memory_space=pltpu.VMEM)
    return pl.pallas_call(
        after_kernel,
        out_shape=jax.ShapeDtypeStruct(value.shape, value.dtype),
        in_specs=[vmem, pl.BlockSpec(memory_space=pl.ANY)],
        out_specs=vmem,
        compiler_params=pltpu.CompilerParams(vmem_limit_bytes=2 * 2**20),
        name="after",
    )(value, earlier)


def on_device(cost_volume, left_image, p_small, p_large):
    index_x, index_y = lax.axis_index("gx"), lax.axis_index("gy")
    here = jnp.stack([index_x % 4, index_y % 4]).astype(jnp.int32)
    numbers = jnp.concatenate([p_small, p_large, here])
    rows = jnp.broadcast_to(jnp.pad(numbers, (0, 6))[:, None], (16, LANES))
    pair, pixel, path = (
        lax.broadcasted_iota(jnp.int32, (32, LANES, 2 * LANES), i) for i in range(3)
    )
    step = 2 * pair + path // LANES
    pick = (pixel == jnp.where(path % LANES < 64, step, LANES - 1 - step)).astype(jnp.bfloat16)
    chips = [[2 * z + c for z in range(16)] for c in range(2)]
    swap = [(i, i ^ 1) for i in range(32)]

    columns = column_message(cost_volume, left_image)
    lines = message(cost_volume, left_image)
    columns = lax.all_to_all(columns, "gy", 0, 0)
    lines = passed_after(lines, columns)
    lines = lax.all_to_all(lines, "gx", 0, 0, axis_index_groups=chips)
    entry_y = path_states(16, 2, False, rows, pick, columns)
    lines = after(lines, entry_y)
    others = lax.ppermute(lines, "gx", swap)

    entry_y = lax.all_to_all(entry_y, "gy", 0, 0)
    entry_x = path_states(32, 0, True, rows, pick, lines, others)
    entry_x = lax.all_to_all(entry_x, "gx", 0, 0, axis_index_groups=chips)

    total, line = replay(columns_replay_kernel, 2, rows, entry_y, cost_volume)
    return replay(lines_replay_kernel, 1, rows, entry_x, total, line)[0]


def solution(mesh):
    in_specs = (P("gy", "gx", None), P("gy", "gx"), P(), P())
    out_specs = P("gy", "gx", None)
    return jax.shard_map(
        on_device, mesh=mesh, in_specs=in_specs, out_specs=out_specs, check_vma=False
    )
```
